32 devices in a mesh: src: 4 (over x, core), tile: 8 (over z, y).
Axes of the slice: x: 2, y: 2, z: 4, core: 2. Of those that a mesh axis runs over, the one named last changes fastest.
Arguments:
- mask_logits: float32 [4096, 512], P('tile'), may hold values from -10 to 10
- target: int32 [4096, 512], P('tile'), may hold values 0 or 1
- weights: float32 [64], P('src'), may hold values from 0.0078125 to 0.03125
- shifts: int32 [64, 2], P('src'), may hold values from -11 to 11
Outputs:
- mask_grad: float32 [4096, 512], P('tile')
- weight_grad: float32 [64], P('src')
- loss: float32 [], replicated
The draws below stay inside these ranges and needn't reach their ends.
All inputs are finite; a program needn't handle non-finite values. No bound on the sum of `target` on one device may be relied on, other than what follows from the above.
Results may differ from the reference program's by a relative error of at most 0.0008.
The reference program's roundings to bfloat16 on the way count: a program that leaves them out, or rounds other values in their place, can miss the bound.
Values may be sent and summed in bfloat16 or wider, within the bound.
A program may use at most 64 MiB of HBM per device.

```python
import math
import jax
import jax.numpy as jnp
from jax import lax

COLS = 512
FREQS = 64
RADIUS = 20
MARGIN = 64
TILE_ROWS = 512
SOURCES = 64
TILES = 8
FRAME = 640
SHIFT = 11
PIXELS = 2097152
N_TILE = 8


def draw_mask_logits(key, part):
    band_rows = TILES * TILE_ROWS
    position = jnp.arange(band_rows, dtype=jnp.float32)[:, None] / band_rows
    noise = jnp.clip(2.0 * jax.random.normal(key, (band_rows, COLS), jnp.float32), -8.0, 8.0)
    trend = -1.5 + 3.0 * position
    return noise + trend


def plant(entries, rng, least, high):
    extent = entries.shape
    index_at = [jax.random.randint(jax.random.fold_in(rng, axis), (), 0, extent[axis]) for axis in range(len(extent))]
    entries = entries.at[tuple(index_at)].set(least)
    longest = extent.index(max(extent))
    index_at[longest] = (index_at[longest] + 1) % extent[longest]
    return entries.at[tuple(index_at)].set(high)


def levels(own_key, dims, cuts, low, largest):
    def one(axis_at, shards_of):
        heights = jax.random.uniform(jax.random.fold_in(jax.random.fold_in(own_key, 6), axis_at), (shards_of,), jnp.float32, low / len(cuts), largest / len(cuts))
        return jnp.repeat(jnp.exp(heights), dims[axis_at] // shards_of).reshape((-1,) + (1,) * (len(dims) - axis_at - 1))

    loudness = one(*cuts[0])
    for cut in cuts[1:]:
        loudness = loudness * one(*cut)
    return loudness


def setup_inputs(seed: int = 0) -> dict:
    key_of = jax.random.split(jax.random.key(seed), 5)
    return {
        "mask_logits": draw_mask_logits(jax.random.fold_in(key_of[4], 71), 0),
        "target": plant((jax.random.randint(key_of[1], (TILES * TILE_ROWS, COLS), 0, 2) < 1).astype(jnp.int32), jax.random.fold_in(key_of[1], 1), 0, 1),
        "weights": jnp.clip(jnp.exp(math.log(0.03125) - 1.3862944 * jax.random.uniform(key_of[2], (SOURCES,), jnp.float32) ** levels(key_of[2], (SOURCES,), ((0, 4),), -0.2, 0.2)), 0.0078125, 0.03125),
        "shifts": plant(jax.random.randint(key_of[3], (SOURCES, 2), 0 - SHIFT, SHIFT + 1), jax.random.fold_in(key_of[3], 1), 0 - SHIFT, SHIFT).astype(jnp.int32),
    }


STEEPNESS = 12.0
THRESHOLD = 0.2
HIGHEST = lax.Precision.HIGHEST


def angles(length_used, offset, period):
    position = jnp.arange(length_used, dtype=jnp.int32)[:, None] + offset
    frequency = jnp.arange(FREQS, dtype=jnp.int32)[None, :] - FREQS // 2
    cycles = jnp.mod(position * frequency, period).astype(jnp.float32)
    angle_value = cycles * jnp.float32(2.0 * 3.141592653589793 / period)
    return jnp.cos(angle_value), jnp.sin(angle_value)


def make_tables(tile_rows, frame_rows, col_count):
    column_cosine, column_sine = angles(col_count, 0, col_count)
    column_forward = jnp.concatenate([column_cosine, -column_sine], 1).astype(jnp.bfloat16)
    frame_cosine, frame_sine = angles(frame_rows, 0, frame_rows)
    row_forward = jnp.concatenate([frame_cosine.T, -frame_sine.T], 0).astype(jnp.bfloat16)
    owned_cosine, owned_sine = angles(tile_rows, MARGIN, frame_rows)
    row_inverse = (jnp.concatenate([owned_cosine, owned_sine], 1) / frame_rows).astype(jnp.bfloat16)
    cosine_scaled = column_cosine.T / col_count
    sine_scaled = column_sine.T / col_count
    upper_block = jnp.concatenate([cosine_scaled, sine_scaled], 1)
    lower_block = jnp.concatenate([-sine_scaled, cosine_scaled], 1)
    column_inverse = jnp.concatenate([upper_block, lower_block], 0).astype(jnp.bfloat16)
    return column_forward, row_forward, row_inverse, column_inverse


def pupil_masks(shifts):
    frequency = jnp.arange(FREQS, dtype=jnp.int32) - FREQS // 2
    offset_across = frequency[None, :, None] - shifts[:, 0][:, None, None]
    offset_along = frequency[None, None, :] - shifts[:, 1][:, None, None]
    inside = offset_across * offset_across + offset_along * offset_along <= RADIUS * RADIUS
    return inside.astype(jnp.float32)


def spectrum(framed, column_forward, row_forward):
    column_part = jnp.dot(framed, column_forward, preferred_element_type=jnp.float32).astype(jnp.bfloat16)
    product = jnp.dot(row_forward, column_part, preferred_element_type=jnp.float32)
    spectrum_real = (product[:FREQS, :FREQS] - product[FREQS:, FREQS:]).astype(jnp.bfloat16)
    spectrum_imag = (product[:FREQS, FREQS:] + product[FREQS:, :FREQS]).astype(jnp.bfloat16)
    return spectrum_real, spectrum_imag


def pupil_blocks(pupils, spectrum_real, spectrum_imag):
    pass_real = pupils * spectrum_real.astype(jnp.float32)
    pass_imag = pupils * spectrum_imag.astype(jnp.float32)
    upper_block = jnp.concatenate([pass_real, pass_imag], 2)
    lower_block = jnp.concatenate([-pass_imag, pass_real], 2)
    return jnp.concatenate([upper_block, lower_block], 1).astype(jnp.bfloat16)


def apply_resist(intensity, target_rows):
    printed = jax.nn.sigmoid(STEEPNESS * (intensity - THRESHOLD))
    error_value = printed - target_rows.astype(jnp.float32)
    cotangent = 2.0 * STEEPNESS * error_value * printed * (1.0 - printed)
    return cotangent, jnp.sum(error_value * error_value)


def frame_gradient(grad_real, grad_imag, column_forward, row_forward):
    upper_block = jnp.concatenate([grad_real, grad_imag], 1)
    lower_block = jnp.concatenate([grad_imag, -grad_real], 1)
    product_grad = jnp.concatenate([upper_block, lower_block], 0)
    column_grad = jnp.dot(row_forward.astype(jnp.float32).T, product_grad, precision=HIGHEST)
    return jnp.dot(column_grad, column_forward.astype(jnp.float32).T, precision=HIGHEST)


def tile_pass(framed, target_rows, weights, pupils, tables):
    column_forward, row_forward, row_inverse, column_inverse = tables
    spectrum_real, spectrum_imag = spectrum(framed, column_forward, row_forward)
    blocks = pupil_blocks(pupils, spectrum_real, spectrum_imag)
    row_field = jnp.einsum('pk,skj->spj', row_inverse.astype(jnp.float32), blocks.astype(jnp.float32), precision=HIGHEST).astype(jnp.bfloat16)
    source_count, tile_rows, doubled_freqs = row_field.shape
    fields = jnp.dot(row_field.reshape(source_count * tile_rows, doubled_freqs), column_inverse, preferred_element_type=jnp.float32)
    fields = fields.reshape(source_count, tile_rows, -1)
    col_count = fields.shape[2] // 2
    powers = fields[:, :, :col_count] * fields[:, :, :col_count] + fields[:, :, col_count:] * fields[:, :, col_count:]
    intensity = jnp.sum(weights[:, None, None] * powers, 0)
    cotangent, error_sum = apply_resist(intensity, target_rows)
    source_terms = jnp.sum(cotangent[None] * powers, axis=(1, 2))
    doubled = jnp.concatenate([cotangent, cotangent], 1)
    scaling = (2.0 * weights)[:, None, None] * doubled[None]
    field_grad = (scaling * fields).astype(jnp.bfloat16)
    row_grad = jnp.dot(field_grad.reshape(source_count * tile_rows, -1), column_inverse.T, preferred_element_type=jnp.float32)
    row_grad = row_grad.astype(jnp.bfloat16).reshape(source_count, tile_rows, -1)
    block_grad = jnp.einsum('pk,spj->skj', row_inverse.astype(jnp.float32), row_grad.astype(jnp.float32), precision=HIGHEST)
    grad_real = jnp.sum(pupils * (block_grad[:, :FREQS, :FREQS] + block_grad[:, FREQS:, FREQS:]), 0)
    grad_imag = jnp.sum(pupils * (block_grad[:, :FREQS, FREQS:] - block_grad[:, FREQS:, :FREQS]), 0)
    return frame_gradient(grad_real, grad_imag, column_forward, row_forward), source_terms, error_sum


def reference(mask_logits, target, weights, shifts):
    opening = jax.nn.sigmoid(mask_logits)
    padded = jnp.pad(opening.astype(jnp.bfloat16), ((MARGIN, MARGIN), (0, 0)))
    tables = make_tables(TILE_ROWS, FRAME, COLS)
    pupils = pupil_masks(shifts)

    def one_tile(tile_index):
        row_start = (tile_index * TILE_ROWS).astype(jnp.int32)
        framed = lax.dynamic_slice_in_dim(padded, row_start, FRAME, 0)
        target_rows = lax.dynamic_slice_in_dim(target, row_start, TILE_ROWS, 0)
        return tile_pass(framed, target_rows, weights, pupils, tables)

    frame_grads, source_terms, error_sums = lax.map(one_tile, jnp.arange(N_TILE, dtype=jnp.int32))
    owned_grads = frame_grads[:, MARGIN:MARGIN + TILE_ROWS]
    owned_grads = owned_grads.at[:-1, TILE_ROWS - MARGIN:].add(frame_grads[1:, :MARGIN])
    owned_grads = owned_grads.at[1:, :MARGIN].add(frame_grads[:-1, MARGIN + TILE_ROWS:])
    mask_grad = owned_grads.reshape(-1, COLS) * opening * (1.0 - opening)
    weight_grad = jnp.sum(source_terms, 0) / PIXELS
    loss = jnp.sum(error_sums) / PIXELS
    return mask_grad, weight_grad, loss
```

```python
import functools

import jax
import jax.numpy as jnp
import ml_dtypes
import numpy as np
from jax import lax
from jax.experimental import pallas as pl
from jax.experimental.pallas import tpu as pltpu
from jax.sharding import PartitionSpec as P

FREQS = 64
RADIUS = 20
MARGIN = 64
STEEPNESS = 12.0
THRESHOLD = 0.2

BOTH = 2 * FREQS
LANES = 128
GROUP = 4
MESH = pl.DeviceIdType.MESH
F32 = jnp.float32
BF16 = jnp.bfloat16


def angles(length_used, offset, period):
    position = np.arange(length_used, dtype=np.int64)[:, None] + offset
    frequency = np.arange(FREQS, dtype=np.int64)[None, :] - FREQS // 2
    cycles = np.mod(position * frequency, period).astype(np.float32)
    value = (cycles * np.float32(2.0 * 3.141592653589793 / period)).astype(np.float64)
    return np.cos(value).astype(np.float32), np.sin(value).astype(np.float32)


def make_tables(tile_rows, frame_rows, col_count):
    def rounded(x):
        return np.asarray(x, np.float32).astype(ml_dtypes.bfloat16)

    column_cosine, column_sine = angles(col_count, 0, col_count)
    column_forward = rounded(np.concatenate([column_cosine, -column_sine], 1))
    frame_cosine, frame_sine = angles(frame_rows, 0, frame_rows)
    row_forward = rounded(np.concatenate([frame_cosine.T, -frame_sine.T], 0))
    owned_cosine, owned_sine = angles(tile_rows, MARGIN, frame_rows)
    row_inverse = rounded(
        np.concatenate([owned_cosine, owned_sine], 1) / np.float32(frame_rows)
    )
    scale = np.float32(col_count)
    cosine_scaled, sine_scaled = column_cosine.T / scale, column_sine.T / scale
    real_part = rounded(np.concatenate([cosine_scaled, -sine_scaled], 0))
    imag_part = rounded(np.concatenate([sine_scaled, cosine_scaled], 0))
    chunks = col_count // LANES
    column_inverse = np.stack(
        [
            np.concatenate(
                [part[:, q * LANES : (q + 1) * LANES] for part in (real_part, imag_part)], 1
            )
            for q in range(chunks)
        ]
    )
    column_adjoint = np.concatenate([column_inverse[q].T for q in range(chunks)], 0)
    return (
        column_forward,
        row_forward,
        row_inverse,
        np.ascontiguousarray(row_inverse.T),
        column_inverse,
        np.ascontiguousarray(column_adjoint),
        np.concatenate([row_forward.T, row_forward.T], 1),
        np.concatenate([column_forward.T, column_forward.T], 0),
    )


def dot(a, b):
    return jnp.dot(a, b, preferred_element_type=F32)


def two_parts(x):
    high = x.astype(BF16)
    low = (x - high.astype(F32)).astype(BF16)
    return jnp.concatenate([high, low], 0)


def kernel(
    n_src,
    n_tile,
    logits_ref,
    target_ref,
    weights_ref,
    shifts_ref,
    cf_ref,
    rf_ref,
    ri_ref,
    rit_ref,
    ci_ref,
    cit_ref,
    rft_ref,
    cft_ref,
    mask_grad_ref,
    weight_grad_ref,
    loss_ref,
    target_buf,
    slope,
    params,
    wide,
    spectra,
    pupils,
    row_fields,
    fields,
    cot,
    field_grads,
    terms,
    shares,
    beside,
    stats,
    target_sem,
    param_send,
    param_recv,
    halo_send,
    halo_recv,
    share_send,
    share_recv,
    beside_send,
    beside_recv,
    stat_send,
    stat_recv,
):
    tile_rows, cols = logits_ref.shape
    local = weights_ref.shape[1]
    sources = local * n_src
    rows = tile_rows // n_src
    chunks = cols // LANES
    src = lax.axis_index("src")
    tile = lax.axis_index("tile")
    my_rows = pl.multiple_of(src * rows, rows)

    barrier = pltpu.get_barrier_semaphore()
    for d in range(1, n_src):
        pl.semaphore_signal(
            barrier, inc=1, device_id={"src": lax.rem(src + d, n_src)}, device_id_type=MESH
        )

    def greet(d, carry):
        pl.semaphore_signal(
            barrier, inc=1, device_id={"tile": lax.rem(tile + d, n_tile)}, device_id_type=MESH
        )
        return carry

    lax.fori_loop(1, n_tile, greet, 0)

    target_copy = pltpu.make_async_copy(
        target_ref.at[pl.ds(my_rows, rows)], target_buf, target_sem
    )
    target_copy.start()

    lane = lax.broadcasted_iota(jnp.int32, (local, LANES), 1)
    diagonal = lax.broadcasted_iota(jnp.int32, (local, local), 0) == lax.broadcasted_iota(
        jnp.int32, (local, local), 1
    )
    weight_column = jnp.sum(
        jnp.where(diagonal, jnp.broadcast_to(weights_ref[...], (local, local)), 0.0),
        axis=1,
        keepdims=True,
    )
    shift_values = shifts_ref[...].astype(F32)
    my_params = pl.ds(pl.multiple_of(src * local, local), local)
    params[my_params, :] = jnp.where(
        lane == 0,
        shift_values[:, 0:1],
        jnp.where(lane == 1, shift_values[:, 1:2], weight_column),
    )

    opening = jax.nn.sigmoid(logits_ref[...])
    slope[...] = opening * (1.0 - opening)
    spectra[MARGIN : MARGIN + tile_rows, :] = dot(opening.astype(BF16), cf_ref[...]).astype(BF16)

    pl.semaphore_wait(barrier, n_src - 1 + n_tile - 1)

    def param_copy(d, owner):
        slot = pl.ds(pl.multiple_of(owner * local, local), local)
        return pltpu.make_async_remote_copy(
            src_ref=params.at[slot],
            dst_ref=params.at[slot],
            send_sem=param_send.at[d],
            recv_sem=param_recv.at[owner],
            device_id={"src": lax.rem(src + d, n_src)},
            device_id_type=MESH,
        )

    for d in range(1, n_src):
        param_copy(d, src).start()

    def halo_copy(side):
        source = tile_rows if side == 0 else MARGIN
        dest = 0 if side == 0 else MARGIN + tile_rows
        return pltpu.make_async_remote_copy(
            src_ref=spectra.at[pl.ds(source, MARGIN)],
            dst_ref=spectra.at[pl.ds(dest, MARGIN)],
            send_sem=halo_send.at[side],
            recv_sem=halo_recv.at[side],
            device_id={"tile": tile + 1 if side == 0 else tile - 1},
            device_id_type=MESH,
        )

    not_first, not_last = tile > 0, tile < n_tile - 1

    @pl.when(not_last)
    def _():
        halo_copy(0).start()

    @pl.when(not_first)
    def _():
        halo_copy(1).start()

    @pl.when(tile == 0)
    def _():
        spectra[0:MARGIN, :] = jnp.zeros((MARGIN, BOTH), BF16)

    @pl.when(tile == n_tile - 1)
    def _():
        spectra[MARGIN + tile_rows :, :] = jnp.zeros((MARGIN, BOTH), BF16)

    for d in range(1, n_src):
        param_copy(d, lax.rem(src + n_src - d, n_src)).wait_recv()

    for k in range(3):
        wide[k] = jnp.broadcast_to(params[:, k : k + 1], (sources, LANES))

    frequency_row = (
        lax.rem(lax.broadcasted_iota(jnp.int32, (FREQS, BOTH), 0), FREQS) - FREQS // 2
    ).astype(F32)
    frequency_lane = (
        lax.rem(lax.broadcasted_iota(jnp.int32, (1, BOTH), 1), FREQS) - FREQS // 2
    ).astype(F32)

    @pl.when(not_first)
    def _():
        halo_copy(0).wait_recv()

    @pl.when(not_last)
    def _():
        halo_copy(1).wait_recv()

    half_sign = jnp.where(lax.broadcasted_iota(jnp.int32, (1, BOTH), 1) < FREQS, 1.0, -1.0)
    product = dot(rf_ref[...], spectra[...])
    turned = pltpu.roll(product, FREQS, 1)
    block_top = product[:FREQS] - half_sign * turned[FREQS:]
    block_low = -product[FREQS:] - half_sign * turned[:FREQS]
    inverse_rows = ri_ref[pl.ds(my_rows, rows), :]

    def row_step(pair, carry):
        blocks = []
        for i in range(2):
            s = pair * 2 + i
            along = frequency_row - wide[0, pl.ds(s, 1), :]
            across = frequency_lane - wide[1, pl.ds(s, 1), :]
            inside = along * along + across * across <= float(RADIUS * RADIUS)
            pupils[s] = jnp.where(inside, 1.0, 0.0)
            blocks.append(
                jnp.concatenate(
                    [jnp.where(inside, block_top, 0.0), jnp.where(inside, block_low, 0.0)], 0
                ).astype(BF16)
            )
        both = dot(inverse_rows, jnp.concatenate(blocks, 1)).astype(BF16)
        for i in range(2):
            start = pl.multiple_of((pair * 2 + i) * rows, rows)
            row_fields[pl.ds(start, rows), :] = both[:, i * BOTH : (i + 1) * BOTH]
        return carry

    lax.fori_loop(0, sources // 2, row_step, 0, unroll=2)

    target_copy.wait()
    span = GROUP * rows
    error_sum = jnp.zeros((1, LANES), F32)
    for q in range(chunks):
        inverse_chunk = ci_ref[q]

        def field_step(group, image, q=q, inverse_chunk=inverse_chunk):
            place = pl.ds(pl.multiple_of(group * span, span), span)
            values = dot(row_fields[place, :], inverse_chunk)
            fields[q, place, :] = values
            real, imag = values[:, :LANES], values[:, LANES:]
            power = real * real + imag * imag
            for i in range(GROUP):
                weight = wide[2, pl.ds(group * GROUP + i, 1), :]
                image = image + weight * power[i * rows : (i + 1) * rows]
            return image

        image = lax.fori_loop(0, sources // GROUP, field_step, jnp.zeros((rows, LANES), F32))
        printed = jax.nn.sigmoid(STEEPNESS * (image - THRESHOLD))
        wanted = target_buf[:, q * LANES : (q + 1) * LANES].astype(F32)
        error = printed - wanted
        cot[q] = 2.0 * STEEPNESS * error * printed * (1.0 - printed)
        error_sum = error_sum + jnp.sum(error * error, axis=0, keepdims=True)

    adjoint_rows = rit_ref[:, pl.ds(my_rows, rows)]

    def grad_step(group, carry):
        place = pl.ds(pl.multiple_of(group * span, span), span)
        for i in range(GROUP):
            s = group * GROUP + i
            doubled_weight = 2.0 * wide[2, pl.ds(s, 1), :]
            total = jnp.zeros((8, LANES), F32)
            for q in range(chunks):
                part = fields[q, pl.ds(pl.multiple_of(s * rows, rows), rows), :]
                real, imag = part[:, :LANES], part[:, LANES:]
                scaling = doubled_weight * cot[q]
                real_grad, imag_grad = scaling * real, scaling * imag
                term = real_grad * real + imag_grad * imag
                total = total + jnp.sum(term.reshape(rows // 8, 8, LANES), axis=0)
                at = slice(i * rows, (i + 1) * rows)
                field_grads[at, 2 * q * LANES : (2 * q + 1) * LANES] = real_grad.astype(BF16)
                field_grads[at, (2 * q + 1) * LANES : (2 * q + 2) * LANES] = imag_grad.astype(BF16)
            terms[pl.ds(s, 1), :] = jnp.sum(total, axis=0, keepdims=True)
        row_grad = dot(field_grads[...], cit_ref[...]).astype(BF16)
        top, low = carry
        for pair in range(GROUP // 2):
            begin = 2 * pair * rows
            block_grad = dot(
                adjoint_rows,
                jnp.concatenate(
                    [row_grad[begin : begin + rows], row_grad[begin + rows : begin + 2 * rows]], 1
                ),
            )
            for i in range(2):
                pupil = pupils[group * GROUP + 2 * pair + i]
                one = block_grad[:, i * BOTH : (i + 1) * BOTH]
                top = top + pupil * one[:FREQS]
                low = low + pupil * one[FREQS:]
        return top, low

    zero = jnp.zeros((FREQS, BOTH), F32)
    top, low = lax.fori_loop(0, sources // GROUP, grad_step, (zero, zero))

    shares[src, 0:FREQS, :] = top + half_sign * pltpu.roll(low, FREQS, 1)
    source_column = jnp.sum(terms[...], axis=1, keepdims=True) / (2.0 * wide[2, :, 0:1])
    source_lane = lax.broadcasted_iota(jnp.int32, (sources, LANES), 1)
    source_row = lax.broadcasted_iota(jnp.int32, (sources, LANES), 0)
    sums = jnp.sum(jnp.where(source_lane == source_row, source_column, 0.0), axis=0, keepdims=True)
    error_total = jnp.sum(error_sum, axis=1, keepdims=True)
    first_lane = lax.broadcasted_iota(jnp.int32, (8, LANES), 1)
    first_row = lax.broadcasted_iota(jnp.int32, (8, LANES), 0)
    shares[src, FREQS : FREQS + 8, :] = jnp.where(
        first_row == 0, sums, jnp.where(first_lane == 0, error_total, 0.0)
    )

    def share_copy(d, owner):
        return pltpu.make_async_remote_copy(
            src_ref=shares.at[owner],
            dst_ref=shares.at[owner],
            send_sem=share_send.at[d],
            recv_sem=share_recv.at[owner],
            device_id={"src": lax.rem(src + d, n_src)},
            device_id_type=MESH,
        )

    for d in range(1, n_src):
        share_copy(d, src).start()
    for d in range(1, n_src):
        share_copy(d, lax.rem(src + n_src - d, n_src)).wait_recv()

    whole = shares[0]
    for i in range(1, n_src):
        whole = whole + shares[i]
    beside[2] = whole[:FREQS]
    stats[tile] = whole[FREQS:]

    def beside_copy(side):
        return pltpu.make_async_remote_copy(
            src_ref=beside.at[2],
            dst_ref=beside.at[side],
            send_sem=beside_send.at[side],
            recv_sem=beside_recv.at[side],
            device_id={"tile": tile + 1 if side == 0 else tile - 1},
            device_id_type=MESH,
        )

    @pl.when(not_last)
    def _():
        beside_copy(0).start()

    @pl.when(not_first)
    def _():
        beside_copy(1).start()

    @pl.when(tile == 0)
    def _():
        beside[0] = jnp.zeros((FREQS, BOTH), F32)

    @pl.when(tile == n_tile - 1)
    def _():
        beside[1] = jnp.zeros((FREQS, BOTH), F32)

    def stat_copy(d, owner):
        return pltpu.make_async_remote_copy(
            src_ref=stats.at[owner],
            dst_ref=stats.at[owner],
            send_sem=stat_send.at[d],
            recv_sem=stat_recv.at[owner],
            device_id={"tile": lax.rem(tile + d, n_tile)},
            device_id_type=MESH,
        )

    def start_stat(d, carry):
        stat_copy(d, tile).start()
        return carry

    lax.fori_loop(1, n_tile, start_stat, 0)

    def doubled(half):
        return two_parts(jnp.concatenate([half, half_sign * pltpu.roll(half, FREQS, 1)], 0))

    frame_rows = tile_rows + 2 * MARGIN
    column_grad = dot(rft_ref[MARGIN : MARGIN + tile_rows, :], doubled(whole[:FREQS]))

    @pl.when(not_first)
    def _():
        beside_copy(0).wait_recv()

    @pl.when(not_last)
    def _():
        beside_copy(1).wait_recv()

    before = dot(rft_ref[frame_rows - MARGIN : frame_rows, :], doubled(beside[0]))
    after = dot(rft_ref[0:MARGIN, :], doubled(beside[1]))
    column_grad = jnp.concatenate(
        [
            column_grad[:MARGIN] + before,
            column_grad[MARGIN : tile_rows - MARGIN],
            column_grad[tile_rows - MARGIN :] + after,
        ],
        0,
    )
    high = column_grad.astype(BF16)
    low_part = (column_grad - high.astype(F32)).astype(BF16)
    mask_grad_ref[...] = (
        dot(jnp.concatenate([high, low_part], 1), cft_ref[...]) * slope[...]
    )

    def wait_stat(d, carry):
        stat_copy(d, lax.rem(tile + n_tile - d, n_tile)).wait_recv()
        return carry

    lax.fori_loop(1, n_tile, wait_stat, 0)
    total = jnp.sum(stats[...], axis=0)
    pixels = float(tile_rows * cols * n_tile)
    picked = lax.broadcasted_iota(jnp.int32, (sources, local), 0) == (
        lax.broadcasted_iota(jnp.int32, (sources, local), 1) + src * local
    )
    total_column = jnp.sum(
        jnp.where(source_lane == source_row, total[0:1, :], 0.0), axis=1, keepdims=True
    )
    weight_grad_ref[...] = (
        jnp.sum(jnp.where(picked, total_column, 0.0), axis=0, keepdims=True) / pixels
    )
    loss_ref[...] = total[1:2, 0:1] / pixels

    for d in range(1, n_src):
        param_copy(d, src).wait_send()
        share_copy(d, src).wait_send()

    @pl.when(not_last)
    def _():
        halo_copy(0).wait_send()
        beside_copy(0).wait_send()

    @pl.when(not_first)
    def _():
        halo_copy(1).wait_send()
        beside_copy(1).wait_send()

    def end_stat(d, carry):
        stat_copy(d, tile).wait_send()
        return carry

    lax.fori_loop(1, n_tile, end_stat, 0)


def on_device(n_src, n_tile, mask_logits, target, weights, shifts):
    tile_rows, cols = mask_logits.shape
    local = weights.shape[0]
    sources = local * n_src
    rows = tile_rows // n_src
    chunks = cols // LANES
    frame_rows = tile_rows + 2 * MARGIN
    tables = make_tables(tile_rows, frame_rows, cols)
    vmem = pl.BlockSpec(memory_space=pltpu.VMEM)
    dma = pltpu.SemaphoreType.DMA
    mask_grad, weight_grad, loss = pl.pallas_call(
        functools.partial(kernel, n_src, n_tile),
        out_shape=(
            jax.ShapeDtypeStruct((tile_rows, cols), F32),
            jax.ShapeDtypeStruct((1, local), F32),
            jax.ShapeDtypeStruct((1, 1), F32),
        ),
        in_specs=[vmem, pl.BlockSpec(memory_space=pl.ANY)] + [vmem] * (2 + len(tables)),
        out_specs=(vmem, vmem, vmem),
        scratch_shapes=[
            pltpu.VMEM((rows, cols), jnp.int32),
            pltpu.VMEM((tile_rows, cols), F32),
            pltpu.VMEM((sources, LANES), F32),
            pltpu.VMEM((3, sources, LANES), F32),
            pltpu.VMEM((frame_rows, BOTH), BF16),
            pltpu.VMEM((sources, FREQS, BOTH), F32),
            pltpu.VMEM((sources * rows, BOTH), BF16),
            pltpu.VMEM((chunks, sources * rows, 2 * LANES), F32),
            pltpu.VMEM((chunks, rows, LANES), F32),
            pltpu.VMEM((GROUP * rows, 2 * cols), BF16),
            pltpu.VMEM((sources, LANES), F32),
            pltpu.VMEM((n_src, FREQS + 8, BOTH), F32),
            pltpu.VMEM((3, FREQS, BOTH), F32),
            pltpu.VMEM((n_tile, 8, LANES), F32),
            dma,
            dma((n_src,)),
            dma((n_src,)),
            dma((2,)),
            dma((2,)),
            dma((n_src,)),
            dma((n_src,)),
            dma((2,)),
            dma((2,)),
            dma((n_tile,)),
            dma((n_tile,)),
        ],
        compiler_params=pltpu.CompilerParams(
            collective_id=0, has_side_effects=True, vmem_limit_bytes=56 * 1024 * 1024
        ),
    )(mask_logits, target, weights.reshape(1, local), shifts, *[jnp.asarray(t) for t in tables])
    return mask_grad, weight_grad.reshape(local), loss.reshape(())


def solution(mesh):
    placed = (P("tile", None), P("tile", None), P("src"), P("src", None))
    return jax.shard_map(
        functools.partial(on_device, mesh.shape["src"], mesh.shape["tile"]),
        mesh=mesh,
        in_specs=placed,
        out_specs=(P("tile", None), P("src"), P()),
        check_vma=False,
    )
```

```python
import functools

import jax
import jax.numpy as jnp
import ml_dtypes
import numpy as np
from jax import lax
from jax.experimental import pallas as pl
from jax.experimental.pallas import tpu as pltpu
from jax.sharding import PartitionSpec as P

FREQS = 64
RADIUS = 20
MARGIN = 64
STEEPNESS = 12.0
THRESHOLD = 0.2

BOTH = 2 * FREQS
LANES = 128
GROUP = 4
MESH = pl.DeviceIdType.MESH
F32 = jnp.float32
BF16 = jnp.bfloat16


def angles(length_used, offset, period):
    position = np.arange(length_used, dtype=np.int64)[:, None] + offset
    frequency = np.arange(FREQS, dtype=np.int64)[None, :] - FREQS // 2
    cycles = np.mod(position * frequency, period).astype(np.float32)
    value = (cycles * np.float32(2.0 * 3.141592653589793 / period)).astype(np.float64)
    return np.cos(value).astype(np.float32), np.sin(value).astype(np.float32)


def make_tables(tile_rows, frame_rows, col_count):
    def rounded(x):
        return np.asarray(x, np.float32).astype(ml_dtypes.bfloat16)

    column_cosine, column_sine = angles(col_count, 0, col_count)
    column_forward = rounded(np.concatenate([column_cosine, -column_sine], 1))
    frame_cosine, frame_sine = angles(frame_rows, 0, frame_rows)
    row_forward = rounded(np.concatenate([frame_cosine.T, -frame_sine.T], 0))
    owned_cosine, owned_sine = angles(tile_rows, MARGIN, frame_rows)
    row_inverse = rounded(
        np.concatenate([owned_cosine, owned_sine], 1) / np.float32(frame_rows)
    )
    scale = np.float32(col_count)
    cosine_scaled, sine_scaled = column_cosine.T / scale, column_sine.T / scale
    real_part = rounded(np.concatenate([cosine_scaled, -sine_scaled], 0))
    imag_part = rounded(np.concatenate([sine_scaled, cosine_scaled], 0))
    chunks = col_count // LANES
    column_inverse = np.stack(
        [
            np.concatenate(
                [part[:, q * LANES : (q + 1) * LANES] for part in (real_part, imag_part)], 1
            )
            for q in range(chunks)
        ]
    )
    column_adjoint = np.concatenate([column_inverse[q].T for q in range(chunks)], 0)
    return (
        column_forward,
        row_forward,
        row_inverse,
        np.ascontiguousarray(row_inverse.T),
        column_inverse,
        np.ascontiguousarray(column_adjoint),
        np.concatenate([row_forward.T, row_forward.T], 1),
        np.concatenate([column_forward.T, column_forward.T], 0),
    )


def dot(a, b):
    return jnp.dot(a, b, preferred_element_type=F32)


def two_parts(x):
    high = x.astype(BF16)
    low = (x - high.astype(F32)).astype(BF16)
    return jnp.concatenate([high, low], 0)


def kernel(
    n_src,
    n_tile,
    logits_hbm,
    target_ref,
    weights_ref,
    shifts_ref,
    cf_hbm,
    rf_hbm,
    ri_hbm,
    rit_hbm,
    ci_hbm,
    cit_hbm,
    rft_hbm,
    column_grad_ref,
    weight_grad_ref,
    loss_ref,
    logits_ref,
    cf_ref,
    rf_ref,
    ri_ref,
    rit_ref,
    ci_ref,
    cit_ref,
    rft_ref,
    target_buf,
    params,
    wide,
    spectra,
    pupils,
    row_fields,
    fields,
    cot,
    even_grads,
    odd_grads,
    terms,
    shares,
    beside,
    stats,
    input_sem,
    target_sem,
    param_send,
    param_recv,
    halo_send,
    halo_recv,
    share_send,
    share_recv,
    beside_send,
    beside_recv,
    stat_send,
    stat_recv,
):
    tile_rows, cols = logits_hbm.shape
    local = weights_ref.shape[1]
    sources = local * n_src
    rows = tile_rows // n_src
    chunks = cols // LANES
    src = lax.axis_index("src")
    tile = lax.axis_index("tile")
    my_rows = pl.multiple_of(src * rows, rows)

    barrier = pltpu.get_barrier_semaphore()
    for d in range(1, n_src):
        pl.semaphore_signal(
            barrier, inc=1, device_id={"src": lax.rem(src + d, n_src)}, device_id_type=MESH
        )

    def greet(d, carry):
        pl.semaphore_signal(
            barrier, inc=1, device_id={"tile": lax.rem(tile + d, n_tile)}, device_id_type=MESH
        )
        return carry

    lax.fori_loop(1, n_tile, greet, 0)

    inputs = [
        pltpu.make_async_copy(source, dest, input_sem.at[i])
        for i, (source, dest) in enumerate(
            [
                (logits_hbm, logits_ref),
                (cf_hbm, cf_ref),
                (rf_hbm, rf_ref),
                (ri_hbm.at[pl.ds(my_rows, rows)], ri_ref),
                (ci_hbm, ci_ref),
                (rit_hbm, rit_ref),
                (cit_hbm, cit_ref),
                (rft_hbm, rft_ref),
            ]
        )
    ]
    for copy in inputs:
        copy.start()
    target_copy = pltpu.make_async_copy(
        target_ref.at[pl.ds(my_rows, rows)], target_buf, target_sem
    )
    target_copy.start()

    lane = lax.broadcasted_iota(jnp.int32, (local, LANES), 1)
    diagonal = lax.broadcasted_iota(jnp.int32, (local, local), 0) == lax.broadcasted_iota(
        jnp.int32, (local, local), 1
    )

    def column(row):
        spread = jnp.where(diagonal, jnp.broadcast_to(row, (local, local)), 0.0)
        return jnp.sum(spread, axis=1, keepdims=True)

    shift_values = shifts_ref[...].astype(F32)
    my_params = pl.ds(pl.multiple_of(src * local, local), local)
    params[my_params, :] = jnp.where(
        lane == 0,
        column(shift_values[0:1, :]),
        jnp.where(lane == 1, column(shift_values[1:2, :]), column(weights_ref[...])),
    )
    pl.semaphore_wait(barrier, n_src - 1 + n_tile - 1)

    def param_copy(d, owner):
        slot = pl.ds(pl.multiple_of(owner * local, local), local)
        return pltpu.make_async_remote_copy(
            src_ref=params.at[slot],
            dst_ref=params.at[slot],
            send_sem=param_send.at[d],
            recv_sem=param_recv.at[owner],
            device_id={"src": lax.rem(src + d, n_src)},
            device_id_type=MESH,
        )

    for d in range(1, n_src):
        param_copy(d, src).start()

    inputs[0].wait()
    inputs[1].wait()
    opening = jax.nn.sigmoid(logits_ref[...]).astype(BF16)
    spectra[MARGIN : MARGIN + tile_rows, :] = dot(opening, cf_ref[...]).astype(BF16)

    def halo_copy(side):
        source = tile_rows if side == 0 else MARGIN
        dest = 0 if side == 0 else MARGIN + tile_rows
        return pltpu.make_async_remote_copy(
            src_ref=spectra.at[pl.ds(source, MARGIN)],
            dst_ref=spectra.at[pl.ds(dest, MARGIN)],
            send_sem=halo_send.at[side],
            recv_sem=halo_recv.at[side],
            device_id={"tile": tile + 1 if side == 0 else tile - 1},
            device_id_type=MESH,
        )

    not_first, not_last = tile > 0, tile < n_tile - 1

    @pl.when(not_last)
    def _():
        halo_copy(0).start()

    @pl.when(not_first)
    def _():
        halo_copy(1).start()

    @pl.when(tile == 0)
    def _():
        spectra[0:MARGIN, :] = jnp.zeros((MARGIN, BOTH), BF16)

    @pl.when(tile == n_tile - 1)
    def _():
        spectra[MARGIN + tile_rows :, :] = jnp.zeros((MARGIN, BOTH), BF16)

    for d in range(1, n_src):
        param_copy(d, lax.rem(src + n_src - d, n_src)).wait_recv()

    for k in range(3):
        wide[k] = jnp.broadcast_to(params[:, k : k + 1], (sources, LANES))

    frequency_row = (
        lax.rem(lax.broadcasted_iota(jnp.int32, (FREQS, BOTH), 0), FREQS) - FREQS // 2
    ).astype(F32)
    frequency_lane = (
        lax.rem(lax.broadcasted_iota(jnp.int32, (1, BOTH), 1), FREQS) - FREQS // 2
    ).astype(F32)

    def pupil_step(s, carry):
        along = frequency_row - wide[0, pl.ds(s, 1), :]
        across = frequency_lane - wide[1, pl.ds(s, 1), :]
        inside = along * along + across * across <= float(RADIUS * RADIUS)
        pupils[s] = jnp.where(inside, 1.0, 0.0)
        return carry

    lax.fori_loop(0, sources, pupil_step, 0, unroll=4)
    for copy in inputs[2:5]:
        copy.wait()

    @pl.when(not_first)
    def _():
        halo_copy(0).wait_recv()

    @pl.when(not_last)
    def _():
        halo_copy(1).wait_recv()

    half_sign = jnp.where(lax.broadcasted_iota(jnp.int32, (1, BOTH), 1) < FREQS, 1.0, -1.0)
    product = dot(rf_ref[...], spectra[...])
    turned = pltpu.roll(product, FREQS, 1)
    block_top = product[:FREQS] - half_sign * turned[FREQS:]
    block_low = -product[FREQS:] - half_sign * turned[:FREQS]
    inverse_rows = ri_ref[...]

    def row_step(pair, carry):
        blocks = []
        for i in range(2):
            pupil = pupils[pair * 2 + i]
            blocks.append(
                jnp.concatenate([pupil * block_top, pupil * block_low], 0).astype(BF16)
            )
        both = dot(inverse_rows, jnp.concatenate(blocks, 1)).astype(BF16)
        for i in range(2):
            start = pl.multiple_of((pair * 2 + i) * rows, rows)
            row_fields[pl.ds(start, rows), :] = both[:, i * BOTH : (i + 1) * BOTH]
        return carry

    lax.fori_loop(0, sources // 2, row_step, 0, unroll=4)

    target_copy.wait()
    span = GROUP * rows
    error_sum = jnp.zeros((1, LANES), F32)
    for q in range(chunks):
        inverse_chunk = ci_ref[q]

        def field_step(group, image, q=q, inverse_chunk=inverse_chunk):
            place = pl.ds(pl.multiple_of(group * span, span), span)
            values = dot(row_fields[place, :], inverse_chunk)
            fields[q, place, :] = values
            real, imag = values[:, :LANES], values[:, LANES:]
            power = real * real + imag * imag
            for i in range(GROUP):
                weight = wide[2, pl.ds(group * GROUP + i, 1), :]
                image = image + weight * power[i * rows : (i + 1) * rows]
            return image

        image = lax.fori_loop(
            0, sources // GROUP, field_step, jnp.zeros((rows, LANES), F32), unroll=4
        )
        printed = jax.nn.sigmoid(STEEPNESS * (image - THRESHOLD))
        wanted = target_buf[:, q * LANES : (q + 1) * LANES].astype(F32)
        error = printed - wanted
        cot[q] = 2.0 * STEEPNESS * error * printed * (1.0 - printed)
        error_sum = error_sum + jnp.sum(error * error, axis=0, keepdims=True)

    for copy in inputs[5:]:
        copy.wait()
    adjoint_rows = rit_ref[:, pl.ds(my_rows, rows)]

    def weigh(group, grads):
        for i in range(GROUP):
            s = group * GROUP + i
            doubled_weight = 2.0 * wide[2, pl.ds(s, 1), :]
            total = jnp.zeros((8, LANES), F32)
            for q in range(chunks):
                part = fields[q, pl.ds(pl.multiple_of(s * rows, rows), rows), :]
                real, imag = part[:, :LANES], part[:, LANES:]
                scaling = doubled_weight * cot[q]
                real_grad, imag_grad = scaling * real, scaling * imag
                term = real_grad * real + imag_grad * imag
                total = total + jnp.sum(term.reshape(rows // 8, 8, LANES), axis=0)
                at = slice(i * rows, (i + 1) * rows)
                grads[at, 2 * q * LANES : (2 * q + 1) * LANES] = real_grad.astype(BF16)
                grads[at, (2 * q + 1) * LANES : (2 * q + 2) * LANES] = imag_grad.astype(BF16)
            terms[s] = total

    def adjoint(group, grads, carry):
        row_grad = dot(grads[...], cit_ref[...]).astype(BF16)
        top, low = carry
        for pair in range(GROUP // 2):
            begin = 2 * pair * rows
            block_grad = dot(
                adjoint_rows,
                jnp.concatenate(
                    [row_grad[begin : begin + rows], row_grad[begin + rows : begin + 2 * rows]], 1
                ),
            )
            for i in range(2):
                pupil = pupils[group * GROUP + 2 * pair + i]
                one = block_grad[:, i * BOTH : (i + 1) * BOTH]
                top = top + pupil * one[:FREQS]
                low = low + pupil * one[FREQS:]
        return top, low

    def grad_step(step, carry):
        weigh(2 * step + 1, odd_grads)
        carry = adjoint(2 * step, even_grads, carry)
        weigh(2 * step + 2, even_grads)
        return adjoint(2 * step + 1, odd_grads, carry)

    groups = sources // GROUP
    zero = jnp.zeros((FREQS, BOTH), F32)
    weigh(0, even_grads)
    carry = lax.fori_loop(0, groups // 2 - 1, grad_step, (zero, zero))
    weigh(groups - 1, odd_grads)
    carry = adjoint(groups - 2, even_grads, carry)
    top, low = adjoint(groups - 1, odd_grads, carry)

    shares[src, 0:FREQS, :] = top + half_sign * pltpu.roll(low, FREQS, 1)
    source_column = jnp.sum(jnp.sum(terms[...], axis=1), axis=1, keepdims=True) / (
        2.0 * wide[2, :, 0:1]
    )
    source_lane = lax.broadcasted_iota(jnp.int32, (sources, LANES), 1)
    source_row = lax.broadcasted_iota(jnp.int32, (sources, LANES), 0)
    sums = jnp.sum(jnp.where(source_lane == source_row, source_column, 0.0), axis=0, keepdims=True)
    error_total = jnp.sum(error_sum, axis=1, keepdims=True)
    first_lane = lax.broadcasted_iota(jnp.int32, (8, LANES), 1)
    first_row = lax.broadcasted_iota(jnp.int32, (8, LANES), 0)
    shares[src, FREQS : FREQS + 8, :] = jnp.where(
        first_row == 0, sums, jnp.where(first_lane == 0, error_total, 0.0)
    )

    def share_copy(d, owner):
        return pltpu.make_async_remote_copy(
            src_ref=shares.at[owner],
            dst_ref=shares.at[owner],
            send_sem=share_send.at[d],
            recv_sem=share_recv.at[owner],
            device_id={"src": lax.rem(src + d, n_src)},
            device_id_type=MESH,
        )

    for d in range(1, n_src):
        share_copy(d, src).start()
    for d in range(1, n_src):
        share_copy(d, lax.rem(src + n_src - d, n_src)).wait_recv()

    whole = shares[0]
    for i in range(1, n_src):
        whole = whole + shares[i]
    beside[2] = whole[:FREQS]
    stats[tile] = whole[FREQS:]

    def beside_copy(side):
        return pltpu.make_async_remote_copy(
            src_ref=beside.at[2],
            dst_ref=beside.at[side],
            send_sem=beside_send.at[side],
            recv_sem=beside_recv.at[side],
            device_id={"tile": tile + 1 if side == 0 else tile - 1},
            device_id_type=MESH,
        )

    @pl.when(not_last)
    def _():
        beside_copy(0).start()

    @pl.when(not_first)
    def _():
        beside_copy(1).start()

    @pl.when(tile == 0)
    def _():
        beside[0] = jnp.zeros((FREQS, BOTH), F32)

    @pl.when(tile == n_tile - 1)
    def _():
        beside[1] = jnp.zeros((FREQS, BOTH), F32)

    def stat_copy(d, owner):
        return pltpu.make_async_remote_copy(
            src_ref=stats.at[owner],
            dst_ref=stats.at[owner],
            send_sem=stat_send.at[d],
            recv_sem=stat_recv.at[owner],
            device_id={"tile": lax.rem(tile + d, n_tile)},
            device_id_type=MESH,
        )

    def start_stat(d, carry):
        stat_copy(d, tile).start()
        return carry

    lax.fori_loop(1, n_tile, start_stat, 0)

    def doubled(half):
        return two_parts(jnp.concatenate([half, half_sign * pltpu.roll(half, FREQS, 1)], 0))

    frame_rows = tile_rows + 2 * MARGIN
    column_grad = dot(rft_ref[MARGIN : MARGIN + tile_rows, :], doubled(whole[:FREQS]))

    @pl.when(not_first)
    def _():
        beside_copy(0).wait_recv()

    @pl.when(not_last)
    def _():
        beside_copy(1).wait_recv()

    before = dot(rft_ref[frame_rows - MARGIN : frame_rows, :], doubled(beside[0]))
    after = dot(rft_ref[0:MARGIN, :], doubled(beside[1]))
    column_grad = jnp.concatenate(
        [
            column_grad[:MARGIN] + before,
            column_grad[MARGIN : tile_rows - MARGIN],
            column_grad[tile_rows - MARGIN :] + after,
        ],
        0,
    )
    high = column_grad.astype(BF16)
    column_grad_ref[:, :BOTH] = high
    column_grad_ref[:, BOTH:] = (column_grad - high.astype(F32)).astype(BF16)

    def wait_stat(d, carry):
        stat_copy(d, lax.rem(tile + n_tile - d, n_tile)).wait_recv()
        return carry

    lax.fori_loop(1, n_tile, wait_stat, 0)
    total = jnp.sum(stats[...], axis=0)
    pixels = float(tile_rows * cols * n_tile)
    picked = lax.broadcasted_iota(jnp.int32, (sources, local), 0) == (
        lax.broadcasted_iota(jnp.int32, (sources, local), 1) + src * local
    )
    total_column = jnp.sum(
        jnp.where(source_lane == source_row, total[0:1, :], 0.0), axis=1, keepdims=True
    )
    weight_grad_ref[...] = (
        jnp.sum(jnp.where(picked, total_column, 0.0), axis=0, keepdims=True) / pixels
    )
    loss_ref[...] = total[1:2, 0:1] / pixels

    for d in range(1, n_src):
        param_copy(d, src).wait_send()
        share_copy(d, src).wait_send()

    @pl.when(not_last)
    def _():
        halo_copy(0).wait_send()
        beside_copy(0).wait_send()

    @pl.when(not_first)
    def _():
        halo_copy(1).wait_send()
        beside_copy(1).wait_send()

    def end_stat(d, carry):
        stat_copy(d, tile).wait_send()
        return carry

    lax.fori_loop(1, n_tile, end_stat, 0)


def last_kernel(column_grad, logits, cft, weight_in, loss_in, mask_grad, weight_grad, loss):
    opening = jax.nn.sigmoid(logits[...])
    mask_grad[...] = dot(column_grad[...], cft[...]) * opening * (1.0 - opening)
    weight_grad[...] = weight_in[...]
    loss[...] = loss_in[...]


def on_device(n_src, n_tile, mask_logits, target, weights, shifts):
    tile_rows, cols = mask_logits.shape
    local = weights.shape[0]
    sources = local * n_src
    rows = tile_rows // n_src
    chunks = cols // LANES
    frame_rows = tile_rows + 2 * MARGIN
    tables = [jnp.asarray(t) for t in make_tables(tile_rows, frame_rows, cols)]
    last_table = tables.pop()
    vmem = pl.BlockSpec(memory_space=pltpu.VMEM)
    hbm = pl.BlockSpec(memory_space=pl.ANY)
    dma = pltpu.SemaphoreType.DMA
    buffers = [pltpu.VMEM(t.shape, BF16) for t in tables]
    buffers[2] = pltpu.VMEM((rows, BOTH), BF16)
    small = (jax.ShapeDtypeStruct((1, local), F32), jax.ShapeDtypeStruct((1, 1), F32))
    column_grad, weight_grad, loss = pl.pallas_call(
        functools.partial(kernel, n_src, n_tile),
        out_shape=(jax.ShapeDtypeStruct((tile_rows, 2 * BOTH), BF16),) + small,
        in_specs=[hbm, hbm, vmem, vmem] + [hbm] * len(tables),
        out_specs=(vmem, vmem, vmem),
        scratch_shapes=[pltpu.VMEM((tile_rows, cols), F32)]
        + buffers
        + [
            pltpu.VMEM((rows, cols), jnp.int32),
            pltpu.VMEM((sources, LANES), F32),
            pltpu.VMEM((3, sources, LANES), F32),
            pltpu.VMEM((frame_rows, BOTH), BF16),
            pltpu.VMEM((sources, FREQS, BOTH), F32),
            pltpu.VMEM((sources * rows, BOTH), BF16),
            pltpu.VMEM((chunks, sources * rows, 2 * LANES), F32),
            pltpu.VMEM((chunks, rows, LANES), F32),
            pltpu.VMEM((GROUP * rows, 2 * cols), BF16),
            pltpu.VMEM((GROUP * rows, 2 * cols), BF16),
            pltpu.VMEM((sources, 8, LANES), F32),
            pltpu.VMEM((n_src, FREQS + 8, BOTH), F32),
            pltpu.VMEM((3, FREQS, BOTH), F32),
            pltpu.VMEM((n_tile, 8, LANES), F32),
            dma((1 + len(tables),)),
            dma,
            dma((n_src,)),
            dma((n_src,)),
            dma((2,)),
            dma((2,)),
            dma((n_src,)),
            dma((n_src,)),
            dma((2,)),
            dma((2,)),
            dma((n_tile,)),
            dma((n_tile,)),
        ],
        compiler_params=pltpu.CompilerParams(
            collective_id=0, has_side_effects=True, vmem_limit_bytes=56 * 1024 * 1024
        ),
    )(mask_logits, target, weights.reshape(1, local), shifts.T, *tables)
    steps = 4
    block = tile_rows // steps
    whole_small = [pl.BlockSpec(x.shape, lambda i: (0, 0)) for x in small]
    mask_grad, weight_grad, loss = pl.pallas_call(
        last_kernel,
        grid=(steps,),
        out_shape=(jax.ShapeDtypeStruct((tile_rows, cols), F32),) + small,
        in_specs=[
            pl.BlockSpec((block, 2 * BOTH), lambda i: (i, 0)),
            pl.BlockSpec((block, cols), lambda i: (i, 0)),
            pl.BlockSpec((2 * BOTH, cols), lambda i: (0, 0)),
        ]
        + whole_small,
        out_specs=tuple([pl.BlockSpec((block, cols), lambda i: (i, 0))] + whole_small),
    )(column_grad, mask_logits, last_table, weight_grad, loss)
    return mask_grad, weight_grad.reshape(local), loss.reshape(())


def solution(mesh):
    placed = (P("tile", None), P("tile", None), P("src"), P("src", None))
    return jax.shard_map(
        functools.partial(on_device, mesh.shape["src"], mesh.shape["tile"]),
        mesh=mesh,
        in_specs=placed,
        out_specs=(P("tile", None), P("src"), P()),
        check_vma=False,
    )
```

```python
import functools

import jax
import jax.numpy as jnp
import ml_dtypes
import numpy as np
from jax import lax
from jax.experimental import pallas as pl
from jax.experimental.pallas import tpu as pltpu
from jax.sharding import PartitionSpec as P

FREQS = 64
RADIUS = 20
MARGIN = 64
STEEPNESS = 12.0
THRESHOLD = 0.2

BOTH = 2 * FREQS
LANES = 128
GROUP = 4
WIDE_GROUP = 8
MESH = pl.DeviceIdType.MESH
F32 = jnp.float32
BF16 = jnp.bfloat16


def angles(length_used, offset, period):
    position = np.arange(length_used, dtype=np.int64)[:, None] + offset
    frequency = np.arange(FREQS, dtype=np.int64)[None, :] - FREQS // 2
    cycles = np.mod(position * frequency, period).astype(np.float32)
    value = (cycles * np.float32(2.0 * 3.141592653589793 / period)).astype(np.float64)
    return np.cos(value).astype(np.float32), np.sin(value).astype(np.float32)


def make_tables(tile_rows, frame_rows, col_count):
    def rounded(x):
        return np.asarray(x, np.float32).astype(ml_dtypes.bfloat16)

    column_cosine, column_sine = angles(col_count, 0, col_count)
    column_forward = rounded(np.concatenate([column_cosine, -column_sine], 1))
    frame_cosine, frame_sine = angles(frame_rows, 0, frame_rows)
    row_forward = rounded(np.concatenate([frame_cosine.T, -frame_sine.T], 0))
    owned_cosine, owned_sine = angles(tile_rows, MARGIN, frame_rows)
    row_inverse = rounded(
        np.concatenate([owned_cosine, owned_sine], 1) / np.float32(frame_rows)
    )
    scale = np.float32(col_count)
    cosine_scaled, sine_scaled = column_cosine.T / scale, column_sine.T / scale
    real_part = rounded(np.concatenate([cosine_scaled, -sine_scaled], 0))
    imag_part = rounded(np.concatenate([sine_scaled, cosine_scaled], 0))
    chunks = col_count // LANES
    column_inverse = np.stack(
        [
            np.concatenate(
                [part[:, q * LANES : (q + 1) * LANES] for part in (real_part, imag_part)], 1
            )
            for q in range(chunks)
        ]
    )
    column_adjoint = np.concatenate([column_inverse[q].T for q in range(chunks)], 0)
    return (
        column_forward,
        row_forward,
        row_inverse,
        np.ascontiguousarray(row_inverse.T),
        column_inverse,
        np.ascontiguousarray(column_adjoint),
        np.concatenate([row_forward.T, row_forward.T], 1),
        np.concatenate([column_forward.T, column_forward.T], 0),
    )


def dot(a, b):
    return jnp.dot(a, b, preferred_element_type=F32)


def two_parts(x):
    high = x.astype(BF16)
    low = (x - high.astype(F32)).astype(BF16)
    return jnp.concatenate([high, low], 0)


def kernel(
    n_src,
    n_tile,
    logits_hbm,
    target_ref,
    weights_ref,
    shifts_ref,
    cf_hbm,
    rf_hbm,
    ri_hbm,
    rit_hbm,
    ci_hbm,
    cit_hbm,
    rft_hbm,
    column_grad_ref,
    weight_grad_ref,
    loss_ref,
    logits_ref,
    cf_ref,
    rf_ref,
    ri_ref,
    rit_ref,
    ci_ref,
    cit_ref,
    rft_ref,
    target_buf,
    params,
    wide,
    spectra,
    pupils,
    row_fields,
    fields,
    cot,
    even_grads,
    odd_grads,
    terms,
    shares,
    beside,
    stats,
    input_sem,
    target_sem,
    param_send,
    param_recv,
    halo_send,
    halo_recv,
    share_send,
    share_recv,
    beside_send,
    beside_recv,
    stat_send,
    stat_recv,
):
    tile_rows, cols = logits_hbm.shape
    local = weights_ref.shape[1]
    sources = local * n_src
    rows = tile_rows // n_src
    chunks = cols // LANES
    src = lax.axis_index("src")
    tile = lax.axis_index("tile")
    my_rows = pl.multiple_of(src * rows, rows)

    barrier = pltpu.get_barrier_semaphore()
    for d in range(1, n_src):
        pl.semaphore_signal(
            barrier, inc=1, device_id={"src": lax.rem(src + d, n_src)}, device_id_type=MESH
        )

    def greet(d, carry):
        pl.semaphore_signal(
            barrier, inc=1, device_id={"tile": lax.rem(tile + d, n_tile)}, device_id_type=MESH
        )
        return carry

    lax.fori_loop(1, n_tile, greet, 0)

    inputs = [
        pltpu.make_async_copy(source, dest, input_sem.at[i])
        for i, (source, dest) in enumerate(
            [
                (logits_hbm, logits_ref),
                (cf_hbm, cf_ref),
                (rf_hbm, rf_ref),
                (ri_hbm.at[pl.ds(my_rows, rows)], ri_ref),
                (ci_hbm, ci_ref),
                (rit_hbm, rit_ref),
                (cit_hbm, cit_ref),
                (rft_hbm, rft_ref),
            ]
        )
    ]
    for copy in inputs:
        copy.start()
    target_copy = pltpu.make_async_copy(
        target_ref.at[pl.ds(my_rows, rows)], target_buf, target_sem
    )
    target_copy.start()

    lane = lax.broadcasted_iota(jnp.int32, (local, LANES), 1)
    diagonal = lax.broadcasted_iota(jnp.int32, (local, local), 0) == lax.broadcasted_iota(
        jnp.int32, (local, local), 1
    )

    def column(row):
        spread = jnp.where(diagonal, jnp.broadcast_to(row, (local, local)), 0.0)
        return jnp.sum(spread, axis=1, keepdims=True)

    shift_values = shifts_ref[...].astype(F32)
    my_params = pl.ds(pl.multiple_of(src * local, local), local)
    params[my_params, :] = jnp.where(
        lane == 0,
        column(shift_values[0:1, :]),
        jnp.where(lane == 1, column(shift_values[1:2, :]), column(weights_ref[...])),
    )
    pl.semaphore_wait(barrier, n_src - 1 + n_tile - 1)

    def param_copy(d, owner):
        slot = pl.ds(pl.multiple_of(owner * local, local), local)
        return pltpu.make_async_remote_copy(
            src_ref=params.at[slot],
            dst_ref=params.at[slot],
            send_sem=param_send.at[d],
            recv_sem=param_recv.at[owner],
            device_id={"src": lax.rem(src + d, n_src)},
            device_id_type=MESH,
        )

    for d in range(1, n_src):
        param_copy(d, src).start()

    inputs[0].wait()
    inputs[1].wait()
    opening = jax.nn.sigmoid(logits_ref[...]).astype(BF16)
    spectra[MARGIN : MARGIN + tile_rows, :] = dot(opening, cf_ref[...]).astype(BF16)

    def halo_copy(side):
        source = tile_rows if side == 0 else MARGIN
        dest = 0 if side == 0 else MARGIN + tile_rows
        return pltpu.make_async_remote_copy(
            src_ref=spectra.at[pl.ds(source, MARGIN)],
            dst_ref=spectra.at[pl.ds(dest, MARGIN)],
            send_sem=halo_send.at[side],
            recv_sem=halo_recv.at[side],
            device_id={"tile": tile + 1 if side == 0 else tile - 1},
            device_id_type=MESH,
        )

    not_first, not_last = tile > 0, tile < n_tile - 1

    @pl.when(not_last)
    def _():
        halo_copy(0).start()

    @pl.when(not_first)
    def _():
        halo_copy(1).start()

    @pl.when(tile == 0)
    def _():
        spectra[0:MARGIN, :] = jnp.zeros((MARGIN, BOTH), BF16)

    @pl.when(tile == n_tile - 1)
    def _():
        spectra[MARGIN + tile_rows :, :] = jnp.zeros((MARGIN, BOTH), BF16)

    for d in range(1, n_src):
        param_copy(d, lax.rem(src + n_src - d, n_src)).wait_recv()

    for k in range(3):
        wide[k] = jnp.broadcast_to(params[:, k : k + 1], (sources, LANES))

    frequency_row = (
        lax.rem(lax.broadcasted_iota(jnp.int32, (FREQS, BOTH), 0), FREQS) - FREQS // 2
    ).astype(F32)
    frequency_lane = (
        lax.rem(lax.broadcasted_iota(jnp.int32, (1, BOTH), 1), FREQS) - FREQS // 2
    ).astype(F32)

    def pupil_step(s, carry):
        along = frequency_row - wide[0, pl.ds(s, 1), :]
        across = frequency_lane - wide[1, pl.ds(s, 1), :]
        inside = along * along + across * across <= float(RADIUS * RADIUS)
        pupils[s] = jnp.where(inside, 1.0, 0.0)
        return carry

    lax.fori_loop(0, sources, pupil_step, 0, unroll=4)
    for copy in inputs[2:5]:
        copy.wait()

    @pl.when(not_first)
    def _():
        halo_copy(0).wait_recv()

    @pl.when(not_last)
    def _():
        halo_copy(1).wait_recv()

    half_sign = jnp.where(lax.broadcasted_iota(jnp.int32, (1, BOTH), 1) < FREQS, 1.0, -1.0)
    product = dot(rf_ref[...], spectra[...])
    turned = pltpu.roll(product, FREQS, 1)
    block_top = product[:FREQS] - half_sign * turned[FREQS:]
    block_low = -product[FREQS:] - half_sign * turned[:FREQS]
    inverse_rows = ri_ref[...]

    def row_step(pair, carry):
        blocks = []
        for i in range(2):
            pupil = pupils[pair * 2 + i]
            blocks.append(
                jnp.concatenate([pupil * block_top, pupil * block_low], 0).astype(BF16)
            )
        both = dot(inverse_rows, jnp.concatenate(blocks, 1)).astype(BF16)
        for i in range(2):
            start = pl.multiple_of((pair * 2 + i) * rows, rows)
            row_fields[pl.ds(start, rows), :] = both[:, i * BOTH : (i + 1) * BOTH]
        return carry

    lax.fori_loop(0, sources // 2, row_step, 0, unroll=8)

    target_copy.wait()
    span = GROUP * rows
    error_sum = jnp.zeros((1, LANES), F32)
    for q in range(chunks):
        inverse_chunk = ci_ref[q]

        def field_step(group, image, q=q, inverse_chunk=inverse_chunk):
            place = pl.ds(pl.multiple_of(group * span, span), span)
            values = dot(row_fields[place, :], inverse_chunk)
            fields[q, place, :] = values
            real, imag = values[:, :LANES], values[:, LANES:]
            power = real * real + imag * imag
            for i in range(GROUP):
                weight = wide[2, pl.ds(group * GROUP + i, 1), :]
                image = image + weight * power[i * rows : (i + 1) * rows]
            return image

        image = lax.fori_loop(
            0, sources // GROUP, field_step, jnp.zeros((rows, LANES), F32), unroll=8
        )
        printed = jax.nn.sigmoid(STEEPNESS * (image - THRESHOLD))
        wanted = target_buf[:, q * LANES : (q + 1) * LANES].astype(F32)
        error = printed - wanted
        cot[q] = 2.0 * STEEPNESS * error * printed * (1.0 - printed)
        error_sum = error_sum + jnp.sum(error * error, axis=0, keepdims=True)

    for copy in inputs[5:]:
        copy.wait()
    adjoint_rows = rit_ref[:, pl.ds(my_rows, rows)]

    def weigh(group, grads):
        for i in range(WIDE_GROUP):
            s = group * WIDE_GROUP + i
            doubled_weight = 2.0 * wide[2, pl.ds(s, 1), :]
            total = jnp.zeros((8, LANES), F32)
            for q in range(chunks):
                part = fields[q, pl.ds(pl.multiple_of(s * rows, rows), rows), :]
                real, imag = part[:, :LANES], part[:, LANES:]
                scaling = doubled_weight * cot[q]
                real_grad, imag_grad = scaling * real, scaling * imag
                term = real_grad * real + imag_grad * imag
                total = total + jnp.sum(term.reshape(rows // 8, 8, LANES), axis=0)
                at = slice(i * rows, (i + 1) * rows)
                grads[at, 2 * q * LANES : (2 * q + 1) * LANES] = real_grad.astype(BF16)
                grads[at, (2 * q + 1) * LANES : (2 * q + 2) * LANES] = imag_grad.astype(BF16)
            terms[s] = total

    def adjoint(group, grads, carry):
        row_grad = dot(grads[...], cit_ref[...]).astype(BF16)
        top, low = carry
        for pair in range(WIDE_GROUP // 2):
            begin = 2 * pair * rows
            block_grad = dot(
                adjoint_rows,
                jnp.concatenate(
                    [row_grad[begin : begin + rows], row_grad[begin + rows : begin + 2 * rows]], 1
                ),
            )
            for i in range(2):
                pupil = pupils[group * WIDE_GROUP + 2 * pair + i]
                one = block_grad[:, i * BOTH : (i + 1) * BOTH]
                top = top + pupil * one[:FREQS]
                low = low + pupil * one[FREQS:]
        return top, low

    def grad_step(step, carry):
        weigh(2 * step + 1, odd_grads)
        carry = adjoint(2 * step, even_grads, carry)
        weigh(2 * step + 2, even_grads)
        return adjoint(2 * step + 1, odd_grads, carry)

    groups = sources // WIDE_GROUP
    zero = jnp.zeros((FREQS, BOTH), F32)
    weigh(0, even_grads)
    carry = lax.fori_loop(0, groups // 2 - 1, grad_step, (zero, zero))
    weigh(groups - 1, odd_grads)
    carry = adjoint(groups - 2, even_grads, carry)
    top, low = adjoint(groups - 1, odd_grads, carry)

    shares[src, 0:FREQS, :] = top + half_sign * pltpu.roll(low, FREQS, 1)
    source_column = jnp.sum(jnp.sum(terms[...], axis=1), axis=1, keepdims=True) / (
        2.0 * wide[2, :, 0:1]
    )
    source_lane = lax.broadcasted_iota(jnp.int32, (sources, LANES), 1)
    source_row = lax.broadcasted_iota(jnp.int32, (sources, LANES), 0)
    sums = jnp.sum(jnp.where(source_lane == source_row, source_column, 0.0), axis=0, keepdims=True)
    error_total = jnp.sum(error_sum, axis=1, keepdims=True)
    first_lane = lax.broadcasted_iota(jnp.int32, (8, LANES), 1)
    first_row = lax.broadcasted_iota(jnp.int32, (8, LANES), 0)
    shares[src, FREQS : FREQS + 8, :] = jnp.where(
        first_row == 0, sums, jnp.where(first_lane == 0, error_total, 0.0)
    )

    def share_copy(d, owner):
        return pltpu.make_async_remote_copy(
            src_ref=shares.at[owner],
            dst_ref=shares.at[owner],
            send_sem=share_send.at[d],
            recv_sem=share_recv.at[owner],
            device_id={"src": lax.rem(src + d, n_src)},
            device_id_type=MESH,
        )

    for d in range(1, n_src):
        share_copy(d, src).start()
    for d in range(1, n_src):
        share_copy(d, lax.rem(src + n_src - d, n_src)).wait_recv()

    whole = shares[0]
    for i in range(1, n_src):
        whole = whole + shares[i]
    beside[2] = whole[:FREQS]
    stats[tile] = whole[FREQS:]

    def beside_copy(side):
        return pltpu.make_async_remote_copy(
            src_ref=beside.at[2],
            dst_ref=beside.at[side],
            send_sem=beside_send.at[side],
            recv_sem=beside_recv.at[side],
            device_id={"tile": tile + 1 if side == 0 else tile - 1},
            device_id_type=MESH,
        )

    @pl.when(not_last)
    def _():
        beside_copy(0).start()

    @pl.when(not_first)
    def _():
        beside_copy(1).start()

    @pl.when(tile == 0)
    def _():
        beside[0] = jnp.zeros((FREQS, BOTH), F32)

    @pl.when(tile == n_tile - 1)
    def _():
        beside[1] = jnp.zeros((FREQS, BOTH), F32)

    def stat_copy(d, owner):
        return pltpu.make_async_remote_copy(
            src_ref=stats.at[owner],
            dst_ref=stats.at[owner],
            send_sem=stat_send.at[d],
            recv_sem=stat_recv.at[owner],
            device_id={"tile": lax.rem(tile + d, n_tile)},
            device_id_type=MESH,
        )

    def start_stat(d, carry):
        stat_copy(d, tile).start()
        return carry

    lax.fori_loop(1, n_tile, start_stat, 0)

    def doubled(half):
        return two_parts(jnp.concatenate([half, half_sign * pltpu.roll(half, FREQS, 1)], 0))

    frame_rows = tile_rows + 2 * MARGIN
    column_grad = dot(rft_ref[MARGIN : MARGIN + tile_rows, :], doubled(whole[:FREQS]))

    @pl.when(not_first)
    def _():
        beside_copy(0).wait_recv()

    @pl.when(not_last)
    def _():
        beside_copy(1).wait_recv()

    before = dot(rft_ref[frame_rows - MARGIN : frame_rows, :], doubled(beside[0]))
    after = dot(rft_ref[0:MARGIN, :], doubled(beside[1]))
    column_grad = jnp.concatenate(
        [
            column_grad[:MARGIN] + before,
            column_grad[MARGIN : tile_rows - MARGIN],
            column_grad[tile_rows - MARGIN :] + after,
        ],
        0,
    )
    high = column_grad.astype(BF16)
    column_grad_ref[:, :BOTH] = high
    column_grad_ref[:, BOTH:] = (column_grad - high.astype(F32)).astype(BF16)

    def wait_stat(d, carry):
        stat_copy(d, lax.rem(tile + n_tile - d, n_tile)).wait_recv()
        return carry

    lax.fori_loop(1, n_tile, wait_stat, 0)
    total = jnp.sum(stats[...], axis=0)
    pixels = float(tile_rows * cols * n_tile)
    picked = lax.broadcasted_iota(jnp.int32, (sources, local), 0) == (
        lax.broadcasted_iota(jnp.int32, (sources, local), 1) + src * local
    )
    total_column = jnp.sum(
        jnp.where(source_lane == source_row, total[0:1, :], 0.0), axis=1, keepdims=True
    )
    weight_grad_ref[...] = (
        jnp.sum(jnp.where(picked, total_column, 0.0), axis=0, keepdims=True) / pixels
    )
    loss_ref[...] = total[1:2, 0:1] / pixels

    for d in range(1, n_src):
        param_copy(d, src).wait_send()
        share_copy(d, src).wait_send()

    @pl.when(not_last)
    def _():
        halo_copy(0).wait_send()
        beside_copy(0).wait_send()

    @pl.when(not_first)
    def _():
        halo_copy(1).wait_send()
        beside_copy(1).wait_send()

    def end_stat(d, carry):
        stat_copy(d, tile).wait_send()
        return carry

    lax.fori_loop(1, n_tile, end_stat, 0)


def on_device(n_src, n_tile, mask_logits, target, weights, shifts):
    tile_rows, cols = mask_logits.shape
    local = weights.shape[0]
    sources = local * n_src
    rows = tile_rows // n_src
    chunks = cols // LANES
    frame_rows = tile_rows + 2 * MARGIN
    tables = [jnp.asarray(t) for t in make_tables(tile_rows, frame_rows, cols)]
    last_table = tables.pop()
    vmem = pl.BlockSpec(memory_space=pltpu.VMEM)
    hbm = pl.BlockSpec(memory_space=pl.ANY)
    dma = pltpu.SemaphoreType.DMA
    buffers = [pltpu.VMEM(t.shape, BF16) for t in tables]
    buffers[2] = pltpu.VMEM((rows, BOTH), BF16)
    small = (jax.ShapeDtypeStruct((1, local), F32), jax.ShapeDtypeStruct((1, 1), F32))
    column_grad, weight_grad, loss = pl.pallas_call(
        functools.partial(kernel, n_src, n_tile),
        out_shape=(jax.ShapeDtypeStruct((tile_rows, 2 * BOTH), BF16),) + small,
        in_specs=[hbm, hbm, vmem, vmem] + [hbm] * len(tables),
        out_specs=(vmem, vmem, vmem),
        scratch_shapes=[pltpu.VMEM((tile_rows, cols), F32)]
        + buffers
        + [
            pltpu.VMEM((rows, cols), jnp.int32),
            pltpu.VMEM((sources, LANES), F32),
            pltpu.VMEM((3, sources, LANES), F32),
            pltpu.VMEM((frame_rows, BOTH), BF16),
            pltpu.VMEM((sources, FREQS, BOTH), F32),
            pltpu.VMEM((sources * rows, BOTH), BF16),
            pltpu.VMEM((chunks, sources * rows, 2 * LANES), F32),
            pltpu.VMEM((chunks, rows, LANES), F32),
            pltpu.VMEM((WIDE_GROUP * rows, 2 * cols), BF16),
            pltpu.VMEM((WIDE_GROUP * rows, 2 * cols), BF16),
            pltpu.VMEM((sources, 8, LANES), F32),
            pltpu.VMEM((n_src, FREQS + 8, BOTH), F32),
            pltpu.VMEM((3, FREQS, BOTH), F32),
            pltpu.VMEM((n_tile, 8, LANES), F32),
            dma((1 + len(tables),)),
            dma,
            dma((n_src,)),
            dma((n_src,)),
            dma((2,)),
            dma((2,)),
            dma((n_src,)),
            dma((n_src,)),
            dma((2,)),
            dma((2,)),
            dma((n_tile,)),
            dma((n_tile,)),
        ],
        compiler_params=pltpu.CompilerParams(
            collective_id=0, has_side_effects=True, vmem_limit_bytes=56 * 1024 * 1024
        ),
    )(mask_logits, target, weights.reshape(1, local), shifts.T, *tables)
    opening = jax.nn.sigmoid(mask_logits)
    mask_grad = dot(column_grad, last_table) * opening * (1.0 - opening)
    return mask_grad, weight_grad.reshape(local), loss.reshape(())


def solution(mesh):
    placed = (P("tile", None), P("tile", None), P("src"), P("src", None))
    return jax.shard_map(
        functools.partial(on_device, mesh.shape["src"], mesh.shape["tile"]),
        mesh=mesh,
        in_specs=placed,
        out_specs=(P("tile", None), P("src"), P()),
        check_vma=False,
    )
```

```python
import functools

import jax
import jax.numpy as jnp
import ml_dtypes
import numpy as np
from jax import lax
from jax.experimental import pallas as pl
from jax.experimental.pallas import tpu as pltpu
from jax.sharding import PartitionSpec as P

FREQS = 64
RADIUS = 20
MARGIN = 64
STEEPNESS = 12.0
THRESHOLD = 0.2

BOTH = 2 * FREQS
LANES = 128
GROUP = 4
WIDE_GROUP = 8
MESH = pl.DeviceIdType.MESH
F32 = jnp.float32
BF16 = jnp.bfloat16


def angles(length_used, offset, period):
    position = np.arange(length_used, dtype=np.int64)[:, None] + offset
    frequency = np.arange(FREQS, dtype=np.int64)[None, :] - FREQS // 2
    cycles = np.mod(position * frequency, period).astype(np.float32)
    value = (cycles * np.float32(2.0 * 3.141592653589793 / period)).astype(np.float64)
    return np.cos(value).astype(np.float32), np.sin(value).astype(np.float32)


def make_tables(tile_rows, frame_rows, col_count):
    def rounded(x):
        return np.asarray(x, np.float32).astype(ml_dtypes.bfloat16)

    column_cosine, column_sine = angles(col_count, 0, col_count)
    column_forward = rounded(np.concatenate([column_cosine, -column_sine], 1))
    frame_cosine, frame_sine = angles(frame_rows, 0, frame_rows)
    row_forward = rounded(np.concatenate([frame_cosine.T, -frame_sine.T], 0))
    owned_cosine, owned_sine = angles(tile_rows, MARGIN, frame_rows)
    row_inverse = rounded(
        np.concatenate([owned_cosine, owned_sine], 1) / np.float32(frame_rows)
    )
    scale = np.float32(col_count)
    cosine_scaled, sine_scaled = column_cosine.T / scale, column_sine.T / scale
    real_part = rounded(np.concatenate([cosine_scaled, -sine_scaled], 0))
    imag_part = rounded(np.concatenate([sine_scaled, cosine_scaled], 0))
    chunks = col_count // LANES
    column_inverse = np.concatenate(
        [
            np.concatenate(
                [part[:, q * LANES : (q + 1) * LANES] for part in (real_part, imag_part)], 1
            )
            for q in range(chunks)
        ],
        1,
    )
    return (
        column_forward,
        row_forward,
        row_inverse,
        np.ascontiguousarray(row_inverse.T),
        column_inverse,
        np.ascontiguousarray(column_inverse.T),
        np.concatenate([row_forward.T, row_forward.T], 1),
        np.concatenate([column_forward.T, column_forward.T], 0),
    )


def dot(a, b):
    return jnp.dot(a, b, preferred_element_type=F32)


def two_parts(x):
    high = x.astype(BF16)
    low = (x - high.astype(F32)).astype(BF16)
    return jnp.concatenate([high, low], 0)


def kernel(
    n_src,
    n_tile,
    logits_hbm,
    target_ref,
    weights_ref,
    shifts_ref,
    cf_hbm,
    rf_hbm,
    ri_hbm,
    rit_hbm,
    ci_hbm,
    cit_hbm,
    rft_hbm,
    column_grad_ref,
    weight_grad_ref,
    loss_ref,
    logits_ref,
    cf_ref,
    rf_ref,
    ri_ref,
    rit_ref,
    ci_ref,
    cit_ref,
    rft_ref,
    target_buf,
    params,
    wide,
    spectra,
    pupils,
    row_fields,
    fields,
    cot,
    even_grads,
    odd_grads,
    terms,
    shares,
    beside,
    stats,
    input_sem,
    target_sem,
    param_send,
    param_recv,
    halo_send,
    halo_recv,
    share_send,
    share_recv,
    beside_send,
    beside_recv,
    stat_send,
    stat_recv,
):
    tile_rows, cols = logits_hbm.shape
    local = weights_ref.shape[1]
    sources = local * n_src
    rows = tile_rows // n_src
    chunks = cols // LANES
    src = lax.axis_index("src")
    tile = lax.axis_index("tile")
    my_rows = pl.multiple_of(src * rows, rows)

    barrier = pltpu.get_barrier_semaphore()
    for d in range(1, n_src):
        pl.semaphore_signal(
            barrier, inc=1, device_id={"src": lax.rem(src + d, n_src)}, device_id_type=MESH
        )

    def greet(d, carry):
        pl.semaphore_signal(
            barrier, inc=1, device_id={"tile": lax.rem(tile + d, n_tile)}, device_id_type=MESH
        )
        return carry

    lax.fori_loop(1, n_tile, greet, 0)

    inputs = [
        pltpu.make_async_copy(source, dest, input_sem.at[i])
        for i, (source, dest) in enumerate(
            [
                (logits_hbm, logits_ref),
                (cf_hbm, cf_ref),
                (rf_hbm, rf_ref),
                (ri_hbm.at[pl.ds(my_rows, rows)], ri_ref),
                (ci_hbm, ci_ref),
                (rit_hbm, rit_ref),
                (cit_hbm, cit_ref),
                (rft_hbm, rft_ref),
            ]
        )
    ]
    for copy in inputs:
        copy.start()
    target_copy = pltpu.make_async_copy(
        target_ref.at[pl.ds(my_rows, rows)], target_buf, target_sem
    )
    target_copy.start()

    lane = lax.broadcasted_iota(jnp.int32, (local, LANES), 1)
    diagonal = lax.broadcasted_iota(jnp.int32, (local, local), 0) == lax.broadcasted_iota(
        jnp.int32, (local, local), 1
    )

    def column(row):
        spread = jnp.where(diagonal, jnp.broadcast_to(row, (local, local)), 0.0)
        return jnp.sum(spread, axis=1, keepdims=True)

    shift_values = shifts_ref[...].astype(F32)
    my_params = pl.ds(pl.multiple_of(src * local, local), local)
    params[my_params, :] = jnp.where(
        lane == 0,
        column(shift_values[0:1, :]),
        jnp.where(lane == 1, column(shift_values[1:2, :]), column(weights_ref[...])),
    )
    pl.semaphore_wait(barrier, n_src - 1 + n_tile - 1)

    def param_copy(d, owner):
        slot = pl.ds(pl.multiple_of(owner * local, local), local)
        return pltpu.make_async_remote_copy(
            src_ref=params.at[slot],
            dst_ref=params.at[slot],
            send_sem=param_send.at[d],
            recv_sem=param_recv.at[owner],
            device_id={"src": lax.rem(src + d, n_src)},
            device_id_type=MESH,
        )

    for d in range(1, n_src):
        param_copy(d, src).start()

    inputs[0].wait()
    inputs[1].wait()
    opening = jax.nn.sigmoid(logits_ref[...]).astype(BF16)
    spectra[MARGIN : MARGIN + tile_rows, :] = dot(opening, cf_ref[...]).astype(BF16)

    def halo_copy(side):
        source = tile_rows if side == 0 else MARGIN
        dest = 0 if side == 0 else MARGIN + tile_rows
        return pltpu.make_async_remote_copy(
            src_ref=spectra.at[pl.ds(source, MARGIN)],
            dst_ref=spectra.at[pl.ds(dest, MARGIN)],
            send_sem=halo_send.at[side],
            recv_sem=halo_recv.at[side],
            device_id={"tile": tile + 1 if side == 0 else tile - 1},
            device_id_type=MESH,
        )

    not_first, not_last = tile > 0, tile < n_tile - 1

    @pl.when(not_last)
    def _():
        halo_copy(0).start()

    @pl.when(not_first)
    def _():
        halo_copy(1).start()

    @pl.when(tile == 0)
    def _():
        spectra[0:MARGIN, :] = jnp.zeros((MARGIN, BOTH), BF16)

    @pl.when(tile == n_tile - 1)
    def _():
        spectra[MARGIN + tile_rows :, :] = jnp.zeros((MARGIN, BOTH), BF16)

    for d in range(1, n_src):
        param_copy(d, lax.rem(src + n_src - d, n_src)).wait_recv()

    for k in range(3):
        wide[k] = jnp.broadcast_to(params[:, k : k + 1], (sources, LANES))

    frequency_row = (
        lax.rem(lax.broadcasted_iota(jnp.int32, (FREQS, BOTH), 0), FREQS) - FREQS // 2
    ).astype(F32)
    frequency_lane = (
        lax.rem(lax.broadcasted_iota(jnp.int32, (1, BOTH), 1), FREQS) - FREQS // 2
    ).astype(F32)

    def pupil_step(s, carry):
        along = frequency_row - wide[0, pl.ds(s, 1), :]
        across = frequency_lane - wide[1, pl.ds(s, 1), :]
        inside = along * along + across * across <= float(RADIUS * RADIUS)
        pupils[s] = jnp.where(inside, 1.0, 0.0)
        return carry

    lax.fori_loop(0, sources, pupil_step, 0, unroll=4)
    for copy in inputs[2:5]:
        copy.wait()

    @pl.when(not_first)
    def _():
        halo_copy(0).wait_recv()

    @pl.when(not_last)
    def _():
        halo_copy(1).wait_recv()

    half_sign = jnp.where(lax.broadcasted_iota(jnp.int32, (1, BOTH), 1) < FREQS, 1.0, -1.0)
    product = dot(rf_ref[...], spectra[...])
    turned = pltpu.roll(product, FREQS, 1)
    block_top = product[:FREQS] - half_sign * turned[FREQS:]
    block_low = -product[FREQS:] - half_sign * turned[:FREQS]
    inverse_rows = ri_ref[...]

    def row_step(group, carry):
        blocks = []
        for i in range(GROUP):
            pupil = pupils[group * GROUP + i]
            blocks.append(
                jnp.concatenate([pupil * block_top, pupil * block_low], 0).astype(BF16)
            )
        together = dot(inverse_rows, jnp.concatenate(blocks, 1)).astype(BF16)
        for i in range(GROUP):
            start = pl.multiple_of((group * GROUP + i) * rows, rows)
            row_fields[pl.ds(start, rows), :] = together[:, i * BOTH : (i + 1) * BOTH]
        return carry

    lax.fori_loop(0, sources // GROUP, row_step, 0, unroll=4)

    span = GROUP * rows
    cot[...] = jnp.zeros(cot.shape, F32)

    def field_step(group, carry):
        place = pl.ds(pl.multiple_of(group * span, span), span)
        values = dot(row_fields[place, :], ci_ref[...])
        weight = [wide[2, pl.ds(group * GROUP + i, 1), :] for i in range(GROUP)]
        for q in range(chunks):
            real = values[:, 2 * q * LANES : (2 * q + 1) * LANES]
            imag = values[:, (2 * q + 1) * LANES : (2 * q + 2) * LANES]
            fields[q, place, :LANES] = real
            fields[q, place, LANES:] = imag
            power = real * real + imag * imag
            image = cot[q]
            for i in range(GROUP):
                image = image + weight[i] * power[i * rows : (i + 1) * rows]
            cot[q] = image
        return carry

    lax.fori_loop(0, sources // GROUP, field_step, 0, unroll=4)

    target_copy.wait()
    error_sum = jnp.zeros((1, LANES), F32)
    for q in range(chunks):
        printed = jax.nn.sigmoid(STEEPNESS * (cot[q] - THRESHOLD))
        wanted = target_buf[:, q * LANES : (q + 1) * LANES].astype(F32)
        error = printed - wanted
        cot[q] = 2.0 * STEEPNESS * error * printed * (1.0 - printed)
        error_sum = error_sum + jnp.sum(error * error, axis=0, keepdims=True)

    for copy in inputs[5:]:
        copy.wait()
    adjoint_rows = rit_ref[:, pl.ds(my_rows, rows)]

    def weigh(group, grads):
        for i in range(WIDE_GROUP):
            s = group * WIDE_GROUP + i
            doubled_weight = 2.0 * wide[2, pl.ds(s, 1), :]
            total = jnp.zeros((8, LANES), F32)
            for q in range(chunks):
                part = fields[q, pl.ds(pl.multiple_of(s * rows, rows), rows), :]
                real, imag = part[:, :LANES], part[:, LANES:]
                scaling = doubled_weight * cot[q]
                real_grad, imag_grad = scaling * real, scaling * imag
                term = real_grad * real + imag_grad * imag
                total = total + jnp.sum(term.reshape(rows // 8, 8, LANES), axis=0)
                at = slice(i * rows, (i + 1) * rows)
                grads[at, 2 * q * LANES : (2 * q + 1) * LANES] = real_grad.astype(BF16)
                grads[at, (2 * q + 1) * LANES : (2 * q + 2) * LANES] = imag_grad.astype(BF16)
            terms[s] = total

    def adjoint(group, grads, carry):
        top, low = carry
        for part in range(WIDE_GROUP // GROUP):
            row_grad = dot(grads[part * span : (part + 1) * span, :], cit_ref[...]).astype(BF16)
            block_grad = dot(
                adjoint_rows,
                jnp.concatenate([row_grad[i * rows : (i + 1) * rows] for i in range(GROUP)], 1),
            )
            for i in range(GROUP):
                pupil = pupils[group * WIDE_GROUP + part * GROUP + i]
                one = block_grad[:, i * BOTH : (i + 1) * BOTH]
                top = top + pupil * one[:FREQS]
                low = low + pupil * one[FREQS:]
        return top, low

    def grad_step(step, carry):
        weigh(2 * step + 1, odd_grads)
        carry = adjoint(2 * step, even_grads, carry)
        weigh(2 * step + 2, even_grads)
        return adjoint(2 * step + 1, odd_grads, carry)

    groups = sources // WIDE_GROUP
    zero = jnp.zeros((FREQS, BOTH), F32)
    weigh(0, even_grads)
    carry = lax.fori_loop(0, groups // 2 - 1, grad_step, (zero, zero))
    weigh(groups - 1, odd_grads)
    carry = adjoint(groups - 2, even_grads, carry)
    top, low = adjoint(groups - 1, odd_grads, carry)

    shares[src, 0:FREQS, :] = top + half_sign * pltpu.roll(low, FREQS, 1)
    source_column = jnp.sum(jnp.sum(terms[...], axis=1), axis=1, keepdims=True) / (
        2.0 * wide[2, :, 0:1]
    )
    source_lane = lax.broadcasted_iota(jnp.int32, (sources, LANES), 1)
    source_row = lax.broadcasted_iota(jnp.int32, (sources, LANES), 0)
    sums = jnp.sum(jnp.where(source_lane == source_row, source_column, 0.0), axis=0, keepdims=True)
    error_total = jnp.sum(error_sum, axis=1, keepdims=True)
    first_lane = lax.broadcasted_iota(jnp.int32, (8, LANES), 1)
    first_row = lax.broadcasted_iota(jnp.int32, (8, LANES), 0)
    shares[src, FREQS : FREQS + 8, :] = jnp.where(
        first_row == 0, sums, jnp.where(first_lane == 0, error_total, 0.0)
    )

    def share_copy(d, owner):
        return pltpu.make_async_remote_copy(
            src_ref=shares.at[owner],
            dst_ref=shares.at[owner],
            send_sem=share_send.at[d],
            recv_sem=share_recv.at[owner],
            device_id={"src": lax.rem(src + d, n_src)},
            device_id_type=MESH,
        )

    for d in range(1, n_src):
        share_copy(d, src).start()
    for d in range(1, n_src):
        share_copy(d, lax.rem(src + n_src - d, n_src)).wait_recv()

    whole = shares[0]
    for i in range(1, n_src):
        whole = whole + shares[i]
    beside[2] = whole[:FREQS]
    stats[tile] = whole[FREQS:]

    def beside_copy(side):
        return pltpu.make_async_remote_copy(
            src_ref=beside.at[2],
            dst_ref=beside.at[side],
            send_sem=beside_send.at[side],
            recv_sem=beside_recv.at[side],
            device_id={"tile": tile + 1 if side == 0 else tile - 1},
            device_id_type=MESH,
        )

    @pl.when(not_last)
    def _():
        beside_copy(0).start()

    @pl.when(not_first)
    def _():
        beside_copy(1).start()

    @pl.when(tile == 0)
    def _():
        beside[0] = jnp.zeros((FREQS, BOTH), F32)

    @pl.when(tile == n_tile - 1)
    def _():
        beside[1] = jnp.zeros((FREQS, BOTH), F32)

    def stat_copy(d, owner):
        return pltpu.make_async_remote_copy(
            src_ref=stats.at[owner],
            dst_ref=stats.at[owner],
            send_sem=stat_send.at[d],
            recv_sem=stat_recv.at[owner],
            device_id={"tile": lax.rem(tile + d, n_tile)},
            device_id_type=MESH,
        )

    def start_stat(d, carry):
        stat_copy(d, tile).start()
        return carry

    lax.fori_loop(1, n_tile, start_stat, 0)

    def doubled(half):
        return two_parts(jnp.concatenate([half, half_sign * pltpu.roll(half, FREQS, 1)], 0))

    frame_rows = tile_rows + 2 * MARGIN
    column_grad = dot(rft_ref[MARGIN : MARGIN + tile_rows, :], doubled(whole[:FREQS]))

    @pl.when(not_first)
    def _():
        beside_copy(0).wait_recv()

    @pl.when(not_last)
    def _():
        beside_copy(1).wait_recv()

    before = dot(rft_ref[frame_rows - MARGIN : frame_rows, :], doubled(beside[0]))
    after = dot(rft_ref[0:MARGIN, :], doubled(beside[1]))
    column_grad = jnp.concatenate(
        [
            column_grad[:MARGIN] + before,
            column_grad[MARGIN : tile_rows - MARGIN],
            column_grad[tile_rows - MARGIN :] + after,
        ],
        0,
    )
    high = column_grad.astype(BF16)
    column_grad_ref[:, :BOTH] = high
    column_grad_ref[:, BOTH:] = (column_grad - high.astype(F32)).astype(BF16)

    def wait_stat(d, carry):
        stat_copy(d, lax.rem(tile + n_tile - d, n_tile)).wait_recv()
        return carry

    lax.fori_loop(1, n_tile, wait_stat, 0)
    total = jnp.sum(stats[...], axis=0)
    pixels = float(tile_rows * cols * n_tile)
    picked = lax.broadcasted_iota(jnp.int32, (sources, local), 0) == (
        lax.broadcasted_iota(jnp.int32, (sources, local), 1) + src * local
    )
    total_column = jnp.sum(
        jnp.where(source_lane == source_row, total[0:1, :], 0.0), axis=1, keepdims=True
    )
    weight_grad_ref[...] = (
        jnp.sum(jnp.where(picked, total_column, 0.0), axis=0, keepdims=True) / pixels
    )
    loss_ref[...] = total[1:2, 0:1] / pixels

    for d in range(1, n_src):
        param_copy(d, src).wait_send()
        share_copy(d, src).wait_send()

    @pl.when(not_last)
    def _():
        halo_copy(0).wait_send()
        beside_copy(0).wait_send()

    @pl.when(not_first)
    def _():
        halo_copy(1).wait_send()
        beside_copy(1).wait_send()

    def end_stat(d, carry):
        stat_copy(d, tile).wait_send()
        return carry

    lax.fori_loop(1, n_tile, end_stat, 0)


def on_device(n_src, n_tile, mask_logits, target, weights, shifts):
    tile_rows, cols = mask_logits.shape
    local = weights.shape[0]
    sources = local * n_src
    rows = tile_rows // n_src
    chunks = cols // LANES
    frame_rows = tile_rows + 2 * MARGIN
    tables = [jnp.asarray(t) for t in make_tables(tile_rows, frame_rows, cols)]
    last_table = tables.pop()
    vmem = pl.BlockSpec(memory_space=pltpu.VMEM)
    hbm = pl.BlockSpec(memory_space=pl.ANY)
    dma = pltpu.SemaphoreType.DMA
    buffers = [pltpu.VMEM(t.shape, BF16) for t in tables]
    buffers[2] = pltpu.VMEM((rows, BOTH), BF16)
    small = (jax.ShapeDtypeStruct((1, local), F32), jax.ShapeDtypeStruct((1, 1), F32))
    column_grad, weight_grad, loss = pl.pallas_call(
        functools.partial(kernel, n_src, n_tile),
        out_shape=(jax.ShapeDtypeStruct((tile_rows, 2 * BOTH), BF16),) + small,
        in_specs=[hbm, hbm, vmem, vmem] + [hbm] * len(tables),
        out_specs=(vmem, vmem, vmem),
        scratch_shapes=[pltpu.VMEM((tile_rows, cols), F32)]
        + buffers
        + [
            pltpu.VMEM((rows, cols), jnp.int32),
            pltpu.VMEM((sources, LANES), F32),
            pltpu.VMEM((3, sources, LANES), F32),
            pltpu.VMEM((frame_rows, BOTH), BF16),
            pltpu.VMEM((sources, FREQS, BOTH), F32),
            pltpu.VMEM((sources * rows, BOTH), BF16),
            pltpu.VMEM((chunks, sources * rows, 2 * LANES), F32),
            pltpu.VMEM((chunks, rows, LANES), F32),
            pltpu.VMEM((WIDE_GROUP * rows, 2 * cols), BF16),
            pltpu.VMEM((WIDE_GROUP * rows, 2 * cols), BF16),
            pltpu.VMEM((sources, 8, LANES), F32),
            pltpu.VMEM((n_src, FREQS + 8, BOTH), F32),
            pltpu.VMEM((3, FREQS, BOTH), F32),
            pltpu.VMEM((n_tile, 8, LANES), F32),
            dma((1 + len(tables),)),
            dma,
            dma((n_src,)),
            dma((n_src,)),
            dma((2,)),
            dma((2,)),
            dma((n_src,)),
            dma((n_src,)),
            dma((2,)),
            dma((2,)),
            dma((n_tile,)),
            dma((n_tile,)),
        ],
        compiler_params=pltpu.CompilerParams(
            collective_id=0, has_side_effects=True, vmem_limit_bytes=56 * 1024 * 1024
        ),
    )(mask_logits, target, weights.reshape(1, local), shifts.T, *tables)
    opening = jax.nn.sigmoid(mask_logits)
    mask_grad = dot(column_grad, last_table) * opening * (1.0 - opening)
    return mask_grad, weight_grad.reshape(local), loss.reshape(())


def solution(mesh):
    placed = (P("tile", None), P("tile", None), P("src"), P("src", None))
    return jax.shard_map(
        functools.partial(on_device, mesh.shape["src"], mesh.shape["tile"]),
        mesh=mesh,
        in_specs=placed,
        out_specs=(P("tile", None), P("src"), P()),
        check_vma=False,
    )
```

```python
import functools

import jax
import jax.numpy as jnp
import ml_dtypes
import numpy as np
from jax import lax
from jax.experimental import pallas as pl
from jax.experimental.pallas import tpu as pltpu
from jax.sharding import PartitionSpec as P

FREQS = 64
RADIUS = 20
MARGIN = 64
STEEPNESS = 12.0
THRESHOLD = 0.2

BOTH = 2 * FREQS
LANES = 128
GROUP = 4
WIDE_GROUP = 8
PIECE = 32
MESH = pl.DeviceIdType.MESH
F32 = jnp.float32
BF16 = jnp.bfloat16


def angles(length_used, offset, period):
    position = np.arange(length_used, dtype=np.int64)[:, None] + offset
    frequency = np.arange(FREQS, dtype=np.int64)[None, :] - FREQS // 2
    cycles = np.mod(position * frequency, period).astype(np.float32)
    value = (cycles * np.float32(2.0 * 3.141592653589793 / period)).astype(np.float64)
    return np.cos(value).astype(np.float32), np.sin(value).astype(np.float32)


def make_tables(tile_rows, frame_rows, col_count):
    def rounded(x):
        return np.asarray(x, np.float32).astype(ml_dtypes.bfloat16)

    column_cosine, column_sine = angles(col_count, 0, col_count)
    column_forward = rounded(np.concatenate([column_cosine, -column_sine], 1))
    frame_cosine, frame_sine = angles(frame_rows, 0, frame_rows)
    row_forward = rounded(np.concatenate([frame_cosine.T, -frame_sine.T], 0))
    owned_cosine, owned_sine = angles(tile_rows, MARGIN, frame_rows)
    row_inverse = rounded(
        np.concatenate([owned_cosine, owned_sine], 1) / np.float32(frame_rows)
    )
    scale = np.float32(col_count)
    cosine_scaled, sine_scaled = column_cosine.T / scale, column_sine.T / scale
    real_part = rounded(np.concatenate([cosine_scaled, -sine_scaled], 0))
    imag_part = rounded(np.concatenate([sine_scaled, cosine_scaled], 0))
    chunks = col_count // LANES
    column_inverse = np.concatenate(
        [
            np.concatenate(
                [part[:, q * LANES : (q + 1) * LANES] for part in (real_part, imag_part)], 1
            )
            for q in range(chunks)
        ],
        1,
    )
    return (
        column_forward,
        row_forward,
        row_inverse,
        np.ascontiguousarray(row_inverse.T),
        column_inverse,
        np.ascontiguousarray(column_inverse.T),
        np.concatenate([row_forward.T, row_forward.T], 1),
        np.concatenate([column_forward.T, column_forward.T], 0),
    )


def dot(a, b):
    return jnp.dot(a, b, preferred_element_type=F32)


def two_parts(x):
    high = x.astype(BF16)
    low = (x - high.astype(F32)).astype(BF16)
    return jnp.concatenate([high, low], 0)


def kernel(
    n_src,
    n_tile,
    logits_hbm,
    target_ref,
    weights_ref,
    shifts_ref,
    cf_hbm,
    rf_hbm,
    ri_hbm,
    rit_hbm,
    ci_hbm,
    cit_hbm,
    rft_hbm,
    column_grad_ref,
    weight_grad_ref,
    loss_ref,
    logits_ref,
    cf_ref,
    rf_ref,
    ri_ref,
    rit_ref,
    ci_ref,
    cit_ref,
    rft_ref,
    target_buf,
    params,
    wide,
    spectra,
    pupils,
    row_fields,
    fields,
    cot,
    even_grads,
    odd_grads,
    terms,
    spectrum_sum,
    shares,
    beside,
    stats,
    input_sem,
    target_sem,
    param_send,
    param_recv,
    halo_send,
    halo_recv,
    share_send,
    share_recv,
    beside_send,
    beside_recv,
    stat_send,
    stat_recv,
):
    tile_rows, cols = logits_hbm.shape
    local = weights_ref.shape[1]
    sources = local * n_src
    rows = tile_rows // n_src
    chunks = cols // LANES
    src = lax.axis_index("src")
    tile = lax.axis_index("tile")
    my_rows = pl.multiple_of(src * rows, rows)

    barrier = pltpu.get_barrier_semaphore()
    for d in range(1, n_src):
        pl.semaphore_signal(
            barrier, inc=1, device_id={"src": lax.rem(src + d, n_src)}, device_id_type=MESH
        )

    def greet(d, carry):
        pl.semaphore_signal(
            barrier, inc=1, device_id={"tile": lax.rem(tile + d, n_tile)}, device_id_type=MESH
        )
        return carry

    lax.fori_loop(1, n_tile, greet, 0)

    inputs = [
        pltpu.make_async_copy(source, dest, input_sem.at[i])
        for i, (source, dest) in enumerate(
            [
                (logits_hbm, logits_ref),
                (cf_hbm, cf_ref),
                (rf_hbm, rf_ref),
                (ri_hbm.at[pl.ds(my_rows, rows)], ri_ref),
                (ci_hbm, ci_ref),
                (rit_hbm, rit_ref),
                (cit_hbm, cit_ref),
                (rft_hbm, rft_ref),
            ]
        )
    ]
    for copy in inputs:
        copy.start()
    target_copy = pltpu.make_async_copy(
        target_ref.at[pl.ds(my_rows, rows)], target_buf, target_sem
    )
    target_copy.start()

    lane = lax.broadcasted_iota(jnp.int32, (local, LANES), 1)
    diagonal = lax.broadcasted_iota(jnp.int32, (local, local), 0) == lax.broadcasted_iota(
        jnp.int32, (local, local), 1
    )

    def column(row):
        spread = jnp.where(diagonal, jnp.broadcast_to(row, (local, local)), 0.0)
        return jnp.sum(spread, axis=1, keepdims=True)

    shift_values = shifts_ref[...].astype(F32)
    my_params = pl.ds(pl.multiple_of(src * local, local), local)
    params[my_params, :] = jnp.where(
        lane == 0,
        column(shift_values[0:1, :]),
        jnp.where(lane == 1, column(shift_values[1:2, :]), column(weights_ref[...])),
    )
    pl.semaphore_wait(barrier, n_src - 1 + n_tile - 1)

    def param_copy(d, owner):
        slot = pl.ds(pl.multiple_of(owner * local, local), local)
        return pltpu.make_async_remote_copy(
            src_ref=params.at[slot],
            dst_ref=params.at[slot],
            send_sem=param_send.at[d],
            recv_sem=param_recv.at[owner],
            device_id={"src": lax.rem(src + d, n_src)},
            device_id_type=MESH,
        )

    for d in range(1, n_src):
        param_copy(d, src).start()

    inputs[0].wait()
    inputs[1].wait()
    opening = jax.nn.sigmoid(logits_ref[...]).astype(BF16)
    spectra[MARGIN : MARGIN + tile_rows, :] = dot(opening, cf_ref[...]).astype(BF16)

    def halo_copy(side):
        source = tile_rows if side == 0 else MARGIN
        dest = 0 if side == 0 else MARGIN + tile_rows
        return pltpu.make_async_remote_copy(
            src_ref=spectra.at[pl.ds(source, MARGIN)],
            dst_ref=spectra.at[pl.ds(dest, MARGIN)],
            send_sem=halo_send.at[side],
            recv_sem=halo_recv.at[side],
            device_id={"tile": tile + 1 if side == 0 else tile - 1},
            device_id_type=MESH,
        )

    not_first, not_last = tile > 0, tile < n_tile - 1

    @pl.when(not_last)
    def _():
        halo_copy(0).start()

    @pl.when(not_first)
    def _():
        halo_copy(1).start()

    @pl.when(tile == 0)
    def _():
        spectra[0:MARGIN, :] = jnp.zeros((MARGIN, BOTH), BF16)

    @pl.when(tile == n_tile - 1)
    def _():
        spectra[MARGIN + tile_rows :, :] = jnp.zeros((MARGIN, BOTH), BF16)

    for d in range(1, n_src):
        param_copy(d, lax.rem(src + n_src - d, n_src)).wait_recv()

    for k in range(3):
        wide[k] = jnp.broadcast_to(params[:, k : k + 1], (sources, LANES))

    frequency_row = (
        lax.rem(lax.broadcasted_iota(jnp.int32, (FREQS, BOTH), 0), FREQS) - FREQS // 2
    ).astype(F32)
    frequency_lane = (
        lax.rem(lax.broadcasted_iota(jnp.int32, (1, BOTH), 1), FREQS) - FREQS // 2
    ).astype(F32)

    def pupil_step(s, carry):
        along = frequency_row - wide[0, pl.ds(s, 1), :]
        across = frequency_lane - wide[1, pl.ds(s, 1), :]
        inside = along * along + across * across <= float(RADIUS * RADIUS)
        pupils[s] = jnp.where(inside, 1.0, 0.0)
        return carry

    lax.fori_loop(0, sources, pupil_step, 0, unroll=4)
    for copy in inputs[2:5]:
        copy.wait()

    @pl.when(not_first)
    def _():
        halo_copy(0).wait_recv()

    @pl.when(not_last)
    def _():
        halo_copy(1).wait_recv()

    half_sign = jnp.where(lax.broadcasted_iota(jnp.int32, (1, BOTH), 1) < FREQS, 1.0, -1.0)
    product = dot(rf_ref[...], spectra[...])
    turned = pltpu.roll(product, FREQS, 1)
    block_top = product[:FREQS] - half_sign * turned[FREQS:]
    block_low = -product[FREQS:] - half_sign * turned[:FREQS]
    inverse_rows = ri_ref[...]

    def row_step(group, carry):
        blocks = []
        for i in range(GROUP):
            pupil = pupils[group * GROUP + i]
            blocks.append(
                jnp.concatenate([pupil * block_top, pupil * block_low], 0).astype(BF16)
            )
        together = dot(inverse_rows, jnp.concatenate(blocks, 1)).astype(BF16)
        for i in range(GROUP):
            start = pl.multiple_of((group * GROUP + i) * rows, rows)
            row_fields[pl.ds(start, rows), :] = together[:, i * BOTH : (i + 1) * BOTH]
        return carry

    lax.fori_loop(0, sources // GROUP, row_step, 0, unroll=4)

    span = GROUP * rows
    cot[...] = jnp.zeros(cot.shape, F32)

    def field_step(group, carry):
        place = pl.ds(pl.multiple_of(group * span, span), span)
        values = dot(row_fields[place, :], ci_ref[...])
        for q in range(chunks):
            fields[q, place, :] = values[:, 2 * q * LANES : 2 * (q + 1) * LANES]
        weight = [wide[2, pl.ds(group * GROUP + i, 1), :] for i in range(GROUP)]
        for q in range(chunks):
            for r in range(0, rows, PIECE):
                image = cot[q, r : r + PIECE, :]
                for i in range(GROUP):
                    start = pl.multiple_of((group * GROUP + i) * rows + r, PIECE)
                    part = fields[q, pl.ds(start, PIECE), :]
                    real, imag = part[:, :LANES], part[:, LANES:]
                    image = image + weight[i] * (real * real + imag * imag)
                cot[q, r : r + PIECE, :] = image
        return carry

    lax.fori_loop(0, sources // GROUP, field_step, 0, unroll=4)

    target_copy.wait()
    error_sum = jnp.zeros((1, LANES), F32)
    for q in range(chunks):
        printed = jax.nn.sigmoid(STEEPNESS * (cot[q] - THRESHOLD))
        wanted = target_buf[:, q * LANES : (q + 1) * LANES].astype(F32)
        error = printed - wanted
        cot[q] = 2.0 * STEEPNESS * error * printed * (1.0 - printed)
        error_sum = error_sum + jnp.sum(error * error, axis=0, keepdims=True)

    for copy in inputs[5:]:
        copy.wait()
    adjoint_rows = rit_ref[:, pl.ds(my_rows, rows)]

    def weigh(group, grads):
        for i in range(WIDE_GROUP):
            s = group * WIDE_GROUP + i
            doubled_weight = 2.0 * wide[2, pl.ds(s, 1), :]
            total = jnp.zeros((8, LANES), F32)
            for q in range(chunks):
                for r in range(0, rows, PIECE):
                    start = pl.multiple_of(s * rows + r, PIECE)
                    part = fields[q, pl.ds(start, PIECE), :]
                    real, imag = part[:, :LANES], part[:, LANES:]
                    scaling = doubled_weight * cot[q, r : r + PIECE, :]
                    real_grad, imag_grad = scaling * real, scaling * imag
                    term = real_grad * real + imag_grad * imag
                    total = total + jnp.sum(term.reshape(PIECE // 8, 8, LANES), axis=0)
                    at = slice(i * rows + r, i * rows + r + PIECE)
                    grads[at, 2 * q * LANES : (2 * q + 1) * LANES] = real_grad.astype(BF16)
                    grads[at, (2 * q + 1) * LANES : (2 * q + 2) * LANES] = imag_grad.astype(BF16)
            terms[s] = total

    def adjoint(group, grads):
        for part in range(WIDE_GROUP // GROUP):
            row_grad = dot(grads[part * span : (part + 1) * span, :], cit_ref[...]).astype(BF16)
            block_grad = dot(
                adjoint_rows,
                jnp.concatenate([row_grad[i * rows : (i + 1) * rows] for i in range(GROUP)], 1),
            )
            for half in range(2):
                at = slice(half * FREQS, (half + 1) * FREQS)
                added = spectrum_sum[at, :]
                for i in range(GROUP):
                    pupil = pupils[group * WIDE_GROUP + part * GROUP + i]
                    added = added + pupil * block_grad[at, i * BOTH : (i + 1) * BOTH]
                spectrum_sum[at, :] = added

    def grad_step(step, carry):
        weigh(2 * step + 1, odd_grads)
        adjoint(2 * step, even_grads)
        weigh(2 * step + 2, even_grads)
        adjoint(2 * step + 1, odd_grads)
        return carry

    groups = sources // WIDE_GROUP
    spectrum_sum[...] = jnp.zeros((BOTH, BOTH), F32)
    weigh(0, even_grads)
    lax.fori_loop(0, groups // 2 - 1, grad_step, 0)
    weigh(groups - 1, odd_grads)
    adjoint(groups - 2, even_grads)
    adjoint(groups - 1, odd_grads)
    top, low = spectrum_sum[:FREQS, :], spectrum_sum[FREQS:, :]

    shares[src, 0:FREQS, :] = top + half_sign * pltpu.roll(low, FREQS, 1)
    source_column = jnp.sum(jnp.sum(terms[...], axis=1), axis=1, keepdims=True) / (
        2.0 * wide[2, :, 0:1]
    )
    source_lane = lax.broadcasted_iota(jnp.int32, (sources, LANES), 1)
    source_row = lax.broadcasted_iota(jnp.int32, (sources, LANES), 0)
    sums = jnp.sum(jnp.where(source_lane == source_row, source_column, 0.0), axis=0, keepdims=True)
    error_total = jnp.sum(error_sum, axis=1, keepdims=True)
    first_lane = lax.broadcasted_iota(jnp.int32, (8, LANES), 1)
    first_row = lax.broadcasted_iota(jnp.int32, (8, LANES), 0)
    shares[src, FREQS : FREQS + 8, :] = jnp.where(
        first_row == 0, sums, jnp.where(first_lane == 0, error_total, 0.0)
    )

    def share_copy(d, owner):
        return pltpu.make_async_remote_copy(
            src_ref=shares.at[owner],
            dst_ref=shares.at[owner],
            send_sem=share_send.at[d],
            recv_sem=share_recv.at[owner],
            device_id={"src": lax.rem(src + d, n_src)},
            device_id_type=MESH,
        )

    for d in range(1, n_src):
        share_copy(d, src).start()
    for d in range(1, n_src):
        share_copy(d, lax.rem(src + n_src - d, n_src)).wait_recv()

    whole = shares[0]
    for i in range(1, n_src):
        whole = whole + shares[i]
    beside[2] = whole[:FREQS]
    stats[tile] = whole[FREQS:]

    def beside_copy(side):
        return pltpu.make_async_remote_copy(
            src_ref=beside.at[2],
            dst_ref=beside.at[side],
            send_sem=beside_send.at[side],
            recv_sem=beside_recv.at[side],
            device_id={"tile": tile + 1 if side == 0 else tile - 1},
            device_id_type=MESH,
        )

    @pl.when(not_last)
    def _():
        beside_copy(0).start()

    @pl.when(not_first)
    def _():
        beside_copy(1).start()

    @pl.when(tile == 0)
    def _():
        beside[0] = jnp.zeros((FREQS, BOTH), F32)

    @pl.when(tile == n_tile - 1)
    def _():
        beside[1] = jnp.zeros((FREQS, BOTH), F32)

    def stat_copy(d, owner):
        return pltpu.make_async_remote_copy(
            src_ref=stats.at[owner],
            dst_ref=stats.at[owner],
            send_sem=stat_send.at[d],
            recv_sem=stat_recv.at[owner],
            device_id={"tile": lax.rem(tile + d, n_tile)},
            device_id_type=MESH,
        )

    def start_stat(d, carry):
        stat_copy(d, tile).start()
        return carry

    lax.fori_loop(1, n_tile, start_stat, 0)

    def doubled(half):
        return two_parts(jnp.concatenate([half, half_sign * pltpu.roll(half, FREQS, 1)], 0))

    frame_rows = tile_rows + 2 * MARGIN
    column_grad = dot(rft_ref[MARGIN : MARGIN + tile_rows, :], doubled(whole[:FREQS]))

    @pl.when(not_first)
    def _():
        beside_copy(0).wait_recv()

    @pl.when(not_last)
    def _():
        beside_copy(1).wait_recv()

    before = dot(rft_ref[frame_rows - MARGIN : frame_rows, :], doubled(beside[0]))
    after = dot(rft_ref[0:MARGIN, :], doubled(beside[1]))
    column_grad = jnp.concatenate(
        [
            column_grad[:MARGIN] + before,
            column_grad[MARGIN : tile_rows - MARGIN],
            column_grad[tile_rows - MARGIN :] + after,
        ],
        0,
    )
    high = column_grad.astype(BF16)
    column_grad_ref[:, :BOTH] = high
    column_grad_ref[:, BOTH:] = (column_grad - high.astype(F32)).astype(BF16)

    def wait_stat(d, carry):
        stat_copy(d, lax.rem(tile + n_tile - d, n_tile)).wait_recv()
        return carry

    lax.fori_loop(1, n_tile, wait_stat, 0)
    total = jnp.sum(stats[...], axis=0)
    pixels = float(tile_rows * cols * n_tile)
    picked = lax.broadcasted_iota(jnp.int32, (sources, local), 0) == (
        lax.broadcasted_iota(jnp.int32, (sources, local), 1) + src * local
    )
    total_column = jnp.sum(
        jnp.where(source_lane == source_row, total[0:1, :], 0.0), axis=1, keepdims=True
    )
    weight_grad_ref[...] = (
        jnp.sum(jnp.where(picked, total_column, 0.0), axis=0, keepdims=True) / pixels
    )
    loss_ref[...] = total[1:2, 0:1] / pixels

    for d in range(1, n_src):
        param_copy(d, src).wait_send()
        share_copy(d, src).wait_send()

    @pl.when(not_last)
    def _():
        halo_copy(0).wait_send()
        beside_copy(0).wait_send()

    @pl.when(not_first)
    def _():
        halo_copy(1).wait_send()
        beside_copy(1).wait_send()

    def end_stat(d, carry):
        stat_copy(d, tile).wait_send()
        return carry

    lax.fori_loop(1, n_tile, end_stat, 0)


def on_device(n_src, n_tile, mask_logits, target, weights, shifts):
    tile_rows, cols = mask_logits.shape
    local = weights.shape[0]
    sources = local * n_src
    rows = tile_rows // n_src
    chunks = cols // LANES
    frame_rows = tile_rows + 2 * MARGIN
    tables = [jnp.asarray(t) for t in make_tables(tile_rows, frame_rows, cols)]
    last_table = tables.pop()
    vmem = pl.BlockSpec(memory_space=pltpu.VMEM)
    hbm = pl.BlockSpec(memory_space=pl.ANY)
    dma = pltpu.SemaphoreType.DMA
    buffers = [pltpu.VMEM(t.shape, BF16) for t in tables]
    buffers[2] = pltpu.VMEM((rows, BOTH), BF16)
    small = (jax.ShapeDtypeStruct((1, local), F32), jax.ShapeDtypeStruct((1, 1), F32))
    column_grad, weight_grad, loss = pl.pallas_call(
        functools.partial(kernel, n_src, n_tile),
        out_shape=(jax.ShapeDtypeStruct((tile_rows, 2 * BOTH), BF16),) + small,
        in_specs=[hbm, hbm, vmem, vmem] + [hbm] * len(tables),
        out_specs=(vmem, vmem, vmem),
        scratch_shapes=[pltpu.VMEM((tile_rows, cols), F32)]
        + buffers
        + [
            pltpu.VMEM((rows, cols), jnp.int32),
            pltpu.VMEM((sources, LANES), F32),
            pltpu.VMEM((3, sources, LANES), F32),
            pltpu.VMEM((frame_rows, BOTH), BF16),
            pltpu.VMEM((sources, FREQS, BOTH), F32),
            pltpu.VMEM((sources * rows, BOTH), BF16),
            pltpu.VMEM((chunks, sources * rows, 2 * LANES), F32),
            pltpu.VMEM((chunks, rows, LANES), F32),
            pltpu.VMEM((WIDE_GROUP * rows, 2 * cols), BF16),
            pltpu.VMEM((WIDE_GROUP * rows, 2 * cols), BF16),
            pltpu.VMEM((sources, 8, LANES), F32),
            pltpu.VMEM((BOTH, BOTH), F32),
            pltpu.VMEM((n_src, FREQS + 8, BOTH), F32),
            pltpu.VMEM((3, FREQS, BOTH), F32),
            pltpu.VMEM((n_tile, 8, LANES), F32),
            dma((1 + len(tables),)),
            dma,
            dma((n_src,)),
            dma((n_src,)),
            dma((2,)),
            dma((2,)),
            dma((n_src,)),
            dma((n_src,)),
            dma((2,)),
            dma((2,)),
            dma((n_tile,)),
            dma((n_tile,)),
        ],
        compiler_params=pltpu.CompilerParams(
            collective_id=0, has_side_effects=True, vmem_limit_bytes=56 * 1024 * 1024
        ),
    )(mask_logits, target, weights.reshape(1, local), shifts.T, *tables)
    opening = jax.nn.sigmoid(mask_logits)
    mask_grad = dot(column_grad, last_table) * opening * (1.0 - opening)
    return mask_grad, weight_grad.reshape(local), loss.reshape(())


def solution(mesh):
    placed = (P("tile", None), P("tile", None), P("src"), P("src", None))
    return jax.shard_map(
        functools.partial(on_device, mesh.shape["src"], mesh.shape["tile"]),
        mesh=mesh,
        in_specs=placed,
        out_specs=(P("tile", None), P("src"), P()),
        check_vma=False,
    )
```

```python
import functools

import jax
import jax.numpy as jnp
import ml_dtypes
import numpy as np
from jax import lax
from jax.experimental import pallas as pl
from jax.experimental.pallas import tpu as pltpu
from jax.sharding import PartitionSpec as P

FREQS = 64
RADIUS = 20
MARGIN = 64
STEEPNESS = 12.0
THRESHOLD = 0.2

BOTH = 2 * FREQS
LANES = 128
GROUP = 4
WIDE_GROUP = 8
MESH = pl.DeviceIdType.MESH
F32 = jnp.float32
BF16 = jnp.bfloat16


def angles(length_used, offset, period):
    position = np.arange(length_used, dtype=np.int64)[:, None] + offset
    frequency = np.arange(FREQS, dtype=np.int64)[None, :] - FREQS // 2
    cycles = np.mod(position * frequency, period).astype(np.float32)
    value = (cycles * np.float32(2.0 * 3.141592653589793 / period)).astype(np.float64)
    return np.cos(value).astype(np.float32), np.sin(value).astype(np.float32)


def make_tables(tile_rows, frame_rows, col_count):
    def rounded(x):
        return np.asarray(x, np.float32).astype(ml_dtypes.bfloat16)

    column_cosine, column_sine = angles(col_count, 0, col_count)
    column_forward = rounded(np.concatenate([column_cosine, -column_sine], 1))
    frame_cosine, frame_sine = angles(frame_rows, 0, frame_rows)
    row_forward = rounded(np.concatenate([frame_cosine.T, -frame_sine.T], 0))
    owned_cosine, owned_sine = angles(tile_rows, MARGIN, frame_rows)
    row_inverse = rounded(
        np.concatenate([owned_cosine, owned_sine], 1) / np.float32(frame_rows)
    )
    scale = np.float32(col_count)
    cosine_scaled, sine_scaled = column_cosine.T / scale, column_sine.T / scale
    real_part = rounded(np.concatenate([cosine_scaled, -sine_scaled], 0))
    imag_part = rounded(np.concatenate([sine_scaled, cosine_scaled], 0))
    chunks = col_count // LANES
    column_inverse = np.concatenate(
        [
            np.concatenate(
                [part[:, q * LANES : (q + 1) * LANES] for part in (real_part, imag_part)], 1
            )
            for q in range(chunks)
        ],
        1,
    )
    return (
        column_forward,
        row_forward,
        row_inverse,
        np.ascontiguousarray(row_inverse.T),
        column_inverse,
        np.ascontiguousarray(column_inverse.T),
        np.concatenate([row_forward.T, row_forward.T], 1),
        np.concatenate([column_forward.T, column_forward.T], 0),
    )


def dot(a, b):
    return jnp.dot(a, b, preferred_element_type=F32)


def two_parts(x):
    high = x.astype(BF16)
    low = (x - high.astype(F32)).astype(BF16)
    return jnp.concatenate([high, low], 0)


def kernel(
    n_src,
    n_tile,
    logits_hbm,
    target_ref,
    weights_ref,
    shifts_ref,
    cf_hbm,
    rf_hbm,
    ri_hbm,
    rit_hbm,
    ci_hbm,
    cit_hbm,
    rft_hbm,
    column_grad_ref,
    weight_grad_ref,
    loss_ref,
    logits_ref,
    cf_ref,
    rf_ref,
    ri_ref,
    rit_ref,
    ci_ref,
    cit_ref,
    rft_ref,
    target_buf,
    params,
    wide,
    spectra,
    pupils,
    row_fields,
    fields,
    cot,
    even_grads,
    odd_grads,
    terms,
    shares,
    beside,
    stats,
    input_sem,
    target_sem,
    param_send,
    param_recv,
    halo_send,
    halo_recv,
    share_send,
    share_recv,
    beside_send,
    beside_recv,
    stat_send,
    stat_recv,
):
    tile_rows, cols = logits_hbm.shape
    local = weights_ref.shape[1]
    sources = local * n_src
    rows = tile_rows // n_src
    chunks = cols // LANES
    src = lax.axis_index("src")
    tile = lax.axis_index("tile")
    my_rows = pl.multiple_of(src * rows, rows)

    barrier = pltpu.get_barrier_semaphore()
    for d in range(1, n_src):
        pl.semaphore_signal(
            barrier, inc=1, device_id={"src": lax.rem(src + d, n_src)}, device_id_type=MESH
        )

    def greet(d, carry):
        pl.semaphore_signal(
            barrier, inc=1, device_id={"tile": lax.rem(tile + d, n_tile)}, device_id_type=MESH
        )
        return carry

    lax.fori_loop(1, n_tile, greet, 0)

    inputs = [
        pltpu.make_async_copy(source, dest, input_sem.at[i])
        for i, (source, dest) in enumerate(
            [
                (logits_hbm, logits_ref),
                (cf_hbm, cf_ref),
                (rf_hbm, rf_ref),
                (ri_hbm.at[pl.ds(my_rows, rows)], ri_ref),
                (ci_hbm, ci_ref),
                (rit_hbm, rit_ref),
                (cit_hbm, cit_ref),
                (rft_hbm, rft_ref),
            ]
        )
    ]
    for copy in inputs:
        copy.start()
    target_copy = pltpu.make_async_copy(
        target_ref.at[pl.ds(my_rows, rows)], target_buf, target_sem
    )
    target_copy.start()

    lane = lax.broadcasted_iota(jnp.int32, (local, LANES), 1)
    diagonal = lax.broadcasted_iota(jnp.int32, (local, local), 0) == lax.broadcasted_iota(
        jnp.int32, (local, local), 1
    )

    def column(row):
        spread = jnp.where(diagonal, jnp.broadcast_to(row, (local, local)), 0.0)
        return jnp.sum(spread, axis=1, keepdims=True)

    shift_values = shifts_ref[...].astype(F32)
    my_params = pl.ds(pl.multiple_of(src * local, local), local)
    params[my_params, :] = jnp.where(
        lane == 0,
        column(shift_values[0:1, :]),
        jnp.where(lane == 1, column(shift_values[1:2, :]), column(weights_ref[...])),
    )
    pl.semaphore_wait(barrier, n_src - 1 + n_tile - 1)

    def param_copy(d, owner):
        slot = pl.ds(pl.multiple_of(owner * local, local), local)
        return pltpu.make_async_remote_copy(
            src_ref=params.at[slot],
            dst_ref=params.at[slot],
            send_sem=param_send.at[d],
            recv_sem=param_recv.at[owner],
            device_id={"src": lax.rem(src + d, n_src)},
            device_id_type=MESH,
        )

    for d in range(1, n_src):
        param_copy(d, src).start()

    inputs[0].wait()
    inputs[1].wait()
    opening = jax.nn.sigmoid(logits_ref[...]).astype(BF16)
    spectra[MARGIN : MARGIN + tile_rows, :] = dot(opening, cf_ref[...]).astype(BF16)

    def halo_copy(side):
        source = tile_rows if side == 0 else MARGIN
        dest = 0 if side == 0 else MARGIN + tile_rows
        return pltpu.make_async_remote_copy(
            src_ref=spectra.at[pl.ds(source, MARGIN)],
            dst_ref=spectra.at[pl.ds(dest, MARGIN)],
            send_sem=halo_send.at[side],
            recv_sem=halo_recv.at[side],
            device_id={"tile": tile + 1 if side == 0 else tile - 1},
            device_id_type=MESH,
        )

    not_first, not_last = tile > 0, tile < n_tile - 1

    @pl.when(not_last)
    def _():
        halo_copy(0).start()

    @pl.when(not_first)
    def _():
        halo_copy(1).start()

    @pl.when(tile == 0)
    def _():
        spectra[0:MARGIN, :] = jnp.zeros((MARGIN, BOTH), BF16)

    @pl.when(tile == n_tile - 1)
    def _():
        spectra[MARGIN + tile_rows :, :] = jnp.zeros((MARGIN, BOTH), BF16)

    for d in range(1, n_src):
        param_copy(d, lax.rem(src + n_src - d, n_src)).wait_recv()

    for k in range(3):
        wide[k] = jnp.broadcast_to(params[:, k : k + 1], (sources, LANES))

    frequency_row = (
        lax.rem(lax.broadcasted_iota(jnp.int32, (FREQS, BOTH), 0), FREQS) - FREQS // 2
    ).astype(F32)
    frequency_lane = (
        lax.rem(lax.broadcasted_iota(jnp.int32, (1, BOTH), 1), FREQS) - FREQS // 2
    ).astype(F32)

    def pupil_step(s, carry):
        along = frequency_row - wide[0, pl.ds(s, 1), :]
        across = frequency_lane - wide[1, pl.ds(s, 1), :]
        inside = along * along + across * across <= float(RADIUS * RADIUS)
        pupils[s] = jnp.where(inside, 1.0, 0.0)
        return carry

    lax.fori_loop(0, sources, pupil_step, 0, unroll=4)
    for copy in inputs[2:5]:
        copy.wait()

    @pl.when(not_first)
    def _():
        halo_copy(0).wait_recv()

    @pl.when(not_last)
    def _():
        halo_copy(1).wait_recv()

    half_sign = jnp.where(lax.broadcasted_iota(jnp.int32, (1, BOTH), 1) < FREQS, 1.0, -1.0)
    product = dot(rf_ref[...], spectra[...])
    turned = pltpu.roll(product, FREQS, 1)
    block_top = product[:FREQS] - half_sign * turned[FREQS:]
    block_low = -product[FREQS:] - half_sign * turned[:FREQS]
    inverse_rows = ri_ref[...]

    def row_step(group, carry):
        blocks = []
        for i in range(GROUP):
            pupil = pupils[group * GROUP + i]
            blocks.append(
                jnp.concatenate([pupil * block_top, pupil * block_low], 0).astype(BF16)
            )
        together = dot(inverse_rows, jnp.concatenate(blocks, 1)).astype(BF16)
        for i in range(GROUP):
            start = pl.multiple_of((group * GROUP + i) * rows, rows)
            row_fields[pl.ds(start, rows), :] = together[:, i * BOTH : (i + 1) * BOTH]
        return carry

    lax.fori_loop(0, sources // GROUP, row_step, 0, unroll=16)

    span = GROUP * rows
    cot[...] = jnp.zeros(cot.shape, F32)

    def field_step(group, carry):
        place = pl.ds(pl.multiple_of(group * span, span), span)
        values = dot(row_fields[place, :], ci_ref[...])
        weight = [wide[2, pl.ds(group * GROUP + i, 1), :] for i in range(GROUP)]
        for q in range(chunks):
            real = values[:, 2 * q * LANES : (2 * q + 1) * LANES]
            imag = values[:, (2 * q + 1) * LANES : (2 * q + 2) * LANES]
            fields[q, place, :LANES] = real
            fields[q, place, LANES:] = imag
            power = real * real + imag * imag
            image = cot[q]
            for i in range(GROUP):
                image = image + weight[i] * power[i * rows : (i + 1) * rows]
            cot[q] = image
        return carry

    lax.fori_loop(0, sources // GROUP, field_step, 0, unroll=8)

    target_copy.wait()
    error_sum = jnp.zeros((1, LANES), F32)
    for q in range(chunks):
        printed = jax.nn.sigmoid(STEEPNESS * (cot[q] - THRESHOLD))
        wanted = target_buf[:, q * LANES : (q + 1) * LANES].astype(F32)
        error = printed - wanted
        cot[q] = 2.0 * STEEPNESS * error * printed * (1.0 - printed)
        error_sum = error_sum + jnp.sum(error * error, axis=0, keepdims=True)

    for copy in inputs[5:]:
        copy.wait()
    adjoint_rows = rit_ref[:, pl.ds(my_rows, rows)]

    def weigh(group, grads):
        for i in range(WIDE_GROUP):
            s = group * WIDE_GROUP + i
            doubled_weight = 2.0 * wide[2, pl.ds(s, 1), :]
            total = jnp.zeros((8, LANES), F32)
            for q in range(chunks):
                part = fields[q, pl.ds(pl.multiple_of(s * rows, rows), rows), :]
                real, imag = part[:, :LANES], part[:, LANES:]
                scaling = doubled_weight * cot[q]
                real_grad, imag_grad = scaling * real, scaling * imag
                term = real_grad * real + imag_grad * imag
                total = total + jnp.sum(term.reshape(rows // 8, 8, LANES), axis=0)
                at = slice(i * rows, (i + 1) * rows)
                grads[at, 2 * q * LANES : (2 * q + 1) * LANES] = real_grad.astype(BF16)
                grads[at, (2 * q + 1) * LANES : (2 * q + 2) * LANES] = imag_grad.astype(BF16)
            terms[s] = total

    def adjoint(group, grads, carry):
        top, low = carry
        for part in range(WIDE_GROUP // GROUP):
            row_grad = dot(grads[part * span : (part + 1) * span, :], cit_ref[...]).astype(BF16)
            block_grad = dot(
                adjoint_rows,
                jnp.concatenate([row_grad[i * rows : (i + 1) * rows] for i in range(GROUP)], 1),
            )
            for i in range(GROUP):
                pupil = pupils[group * WIDE_GROUP + part * GROUP + i]
                one = block_grad[:, i * BOTH : (i + 1) * BOTH]
                top = top + pupil * one[:FREQS]
                low = low + pupil * one[FREQS:]
        return top, low

    def grad_step(step, carry):
        weigh(2 * step + 1, odd_grads)
        carry = adjoint(2 * step, even_grads, carry)
        weigh(2 * step + 2, even_grads)
        return adjoint(2 * step + 1, odd_grads, carry)

    groups = sources // WIDE_GROUP
    zero = jnp.zeros((FREQS, BOTH), F32)
    weigh(0, even_grads)
    carry = lax.fori_loop(0, groups // 2 - 1, grad_step, (zero, zero))
    weigh(groups - 1, odd_grads)
    carry = adjoint(groups - 2, even_grads, carry)
    top, low = adjoint(groups - 1, odd_grads, carry)

    shares[src, 0:FREQS, :] = top + half_sign * pltpu.roll(low, FREQS, 1)
    source_column = jnp.sum(jnp.sum(terms[...], axis=1), axis=1, keepdims=True) / (
        2.0 * wide[2, :, 0:1]
    )
    source_lane = lax.broadcasted_iota(jnp.int32, (sources, LANES), 1)
    source_row = lax.broadcasted_iota(jnp.int32, (sources, LANES), 0)
    sums = jnp.sum(jnp.where(source_lane == source_row, source_column, 0.0), axis=0, keepdims=True)
    error_total = jnp.sum(error_sum, axis=1, keepdims=True)
    first_lane = lax.broadcasted_iota(jnp.int32, (8, LANES), 1)
    first_row = lax.broadcasted_iota(jnp.int32, (8, LANES), 0)
    shares[src, FREQS : FREQS + 8, :] = jnp.where(
        first_row == 0, sums, jnp.where(first_lane == 0, error_total, 0.0)
    )

    def share_copy(d, owner):
        return pltpu.make_async_remote_copy(
            src_ref=shares.at[owner],
            dst_ref=shares.at[owner],
            send_sem=share_send.at[d],
            recv_sem=share_recv.at[owner],
            device_id={"src": lax.rem(src + d, n_src)},
            device_id_type=MESH,
        )

    for d in range(1, n_src):
        share_copy(d, src).start()
    for d in range(1, n_src):
        share_copy(d, lax.rem(src + n_src - d, n_src)).wait_recv()

    whole = shares[0]
    for i in range(1, n_src):
        whole = whole + shares[i]
    beside[2] = whole[:FREQS]
    stats[tile] = whole[FREQS:]

    def beside_copy(side):
        return pltpu.make_async_remote_copy(
            src_ref=beside.at[2],
            dst_ref=beside.at[side],
            send_sem=beside_send.at[side],
            recv_sem=beside_recv.at[side],
            device_id={"tile": tile + 1 if side == 0 else tile - 1},
            device_id_type=MESH,
        )

    @pl.when(not_last)
    def _():
        beside_copy(0).start()

    @pl.when(not_first)
    def _():
        beside_copy(1).start()

    @pl.when(tile == 0)
    def _():
        beside[0] = jnp.zeros((FREQS, BOTH), F32)

    @pl.when(tile == n_tile - 1)
    def _():
        beside[1] = jnp.zeros((FREQS, BOTH), F32)

    def stat_copy(d, owner):
        return pltpu.make_async_remote_copy(
            src_ref=stats.at[owner],
            dst_ref=stats.at[owner],
            send_sem=stat_send.at[d],
            recv_sem=stat_recv.at[owner],
            device_id={"tile": lax.rem(tile + d, n_tile)},
            device_id_type=MESH,
        )

    def start_stat(d, carry):
        stat_copy(d, tile).start()
        return carry

    lax.fori_loop(1, n_tile, start_stat, 0)

    def doubled(half):
        return two_parts(jnp.concatenate([half, half_sign * pltpu.roll(half, FREQS, 1)], 0))

    frame_rows = tile_rows + 2 * MARGIN
    column_grad = dot(rft_ref[MARGIN : MARGIN + tile_rows, :], doubled(whole[:FREQS]))

    @pl.when(not_first)
    def _():
        beside_copy(0).wait_recv()

    @pl.when(not_last)
    def _():
        beside_copy(1).wait_recv()

    before = dot(rft_ref[frame_rows - MARGIN : frame_rows, :], doubled(beside[0]))
    after = dot(rft_ref[0:MARGIN, :], doubled(beside[1]))
    column_grad = jnp.concatenate(
        [
            column_grad[:MARGIN] + before,
            column_grad[MARGIN : tile_rows - MARGIN],
            column_grad[tile_rows - MARGIN :] + after,
        ],
        0,
    )
    high = column_grad.astype(BF16)
    column_grad_ref[:, :BOTH] = high
    column_grad_ref[:, BOTH:] = (column_grad - high.astype(F32)).astype(BF16)

    def wait_stat(d, carry):
        stat_copy(d, lax.rem(tile + n_tile - d, n_tile)).wait_recv()
        return carry

    lax.fori_loop(1, n_tile, wait_stat, 0)
    total = jnp.sum(stats[...], axis=0)
    pixels = float(tile_rows * cols * n_tile)
    picked = lax.broadcasted_iota(jnp.int32, (sources, local), 0) == (
        lax.broadcasted_iota(jnp.int32, (sources, local), 1) + src * local
    )
    total_column = jnp.sum(
        jnp.where(source_lane == source_row, total[0:1, :], 0.0), axis=1, keepdims=True
    )
    weight_grad_ref[...] = (
        jnp.sum(jnp.where(picked, total_column, 0.0), axis=0, keepdims=True) / pixels
    )
    loss_ref[...] = total[1:2, 0:1] / pixels

    for d in range(1, n_src):
        param_copy(d, src).wait_send()
        share_copy(d, src).wait_send()

    @pl.when(not_last)
    def _():
        halo_copy(0).wait_send()
        beside_copy(0).wait_send()

    @pl.when(not_first)
    def _():
        halo_copy(1).wait_send()
        beside_copy(1).wait_send()

    def end_stat(d, carry):
        stat_copy(d, tile).wait_send()
        return carry

    lax.fori_loop(1, n_tile, end_stat, 0)


def on_device(n_src, n_tile, mask_logits, target, weights, shifts):
    tile_rows, cols = mask_logits.shape
    local = weights.shape[0]
    sources = local * n_src
    rows = tile_rows // n_src
    chunks = cols // LANES
    frame_rows = tile_rows + 2 * MARGIN
    tables = [jnp.asarray(t) for t in make_tables(tile_rows, frame_rows, cols)]
    last_table = tables.pop()
    vmem = pl.BlockSpec(memory_space=pltpu.VMEM)
    hbm = pl.BlockSpec(memory_space=pl.ANY)
    dma = pltpu.SemaphoreType.DMA
    buffers = [pltpu.VMEM(t.shape, BF16) for t in tables]
    buffers[2] = pltpu.VMEM((rows, BOTH), BF16)
    small = (jax.ShapeDtypeStruct((1, local), F32), jax.ShapeDtypeStruct((1, 1), F32))
    column_grad, weight_grad, loss = pl.pallas_call(
        functools.partial(kernel, n_src, n_tile),
        out_shape=(jax.ShapeDtypeStruct((tile_rows, 2 * BOTH), BF16),) + small,
        in_specs=[hbm, hbm, vmem, vmem] + [hbm] * len(tables),
        out_specs=(vmem, vmem, vmem),
        scratch_shapes=[pltpu.VMEM((tile_rows, cols), F32)]
        + buffers
        + [
            pltpu.VMEM((rows, cols), jnp.int32),
            pltpu.VMEM((sources, LANES), F32),
            pltpu.VMEM((3, sources, LANES), F32),
            pltpu.VMEM((frame_rows, BOTH), BF16),
            pltpu.VMEM((sources, FREQS, BOTH), F32),
            pltpu.VMEM((sources * rows, BOTH), BF16),
            pltpu.VMEM((chunks, sources * rows, 2 * LANES), F32),
            pltpu.VMEM((chunks, rows, LANES), F32),
            pltpu.VMEM((WIDE_GROUP * rows, 2 * cols), BF16),
            pltpu.VMEM((WIDE_GROUP * rows, 2 * cols), BF16),
            pltpu.VMEM((sources, 8, LANES), F32),
            pltpu.VMEM((n_src, FREQS + 8, BOTH), F32),
            pltpu.VMEM((3, FREQS, BOTH), F32),
            pltpu.VMEM((n_tile, 8, LANES), F32),
            dma((1 + len(tables),)),
            dma,
            dma((n_src,)),
            dma((n_src,)),
            dma((2,)),
            dma((2,)),
            dma((n_src,)),
            dma((n_src,)),
            dma((2,)),
            dma((2,)),
            dma((n_tile,)),
            dma((n_tile,)),
        ],
        compiler_params=pltpu.CompilerParams(
            collective_id=0, has_side_effects=True, vmem_limit_bytes=56 * 1024 * 1024
        ),
    )(mask_logits, target, weights.reshape(1, local), shifts.T, *tables)
    opening = jax.nn.sigmoid(mask_logits)
    mask_grad = dot(column_grad, last_table) * opening * (1.0 - opening)
    return mask_grad, weight_grad.reshape(local), loss.reshape(())


def solution(mesh):
    placed = (P("tile", None), P("tile", None), P("src"), P("src", None))
    return jax.shard_map(
        functools.partial(on_device, mesh.shape["src"], mesh.shape["tile"]),
        mesh=mesh,
        in_specs=placed,
        out_specs=(P("tile", None), P("src"), P()),
        check_vma=False,
    )
```
